32 devices in a mesh: row: 4 (over z), col: 8 (over y, x, core).
Axes of the slice: x: 2, y: 2, z: 4, core: 2. Of those that a mesh axis runs over, the one named last changes fastest.
Arguments:
- layer_inputs: float32 [512, 16384], P(('row', 'col')), may hold values from -60 to 60
Outputs:
- gram: float32 [16384, 16384], P('row', 'col')
The draws below stay inside these ranges and needn't reach their ends.
All inputs are finite; a program needn't handle non-finite values.
Results may differ from the reference program's by a relative error of at most 0.000073.
Values sent between devices are 32-bit elements; how exact they have to be, the bound alone decides.
A program may use at most 128 MiB of HBM per device.

```python
import math
import jax
import jax.numpy as jnp
from jax import lax

D = 16384
TOKENS = 512


def draw_layer_inputs(key, part):
    first, second, third = jax.random.split(key, 3)
    base = jnp.clip(jax.random.normal(first, (TOKENS, D), jnp.float32), -6.0, 6.0)
    feature_scale = jnp.exp(jax.random.uniform(third, (D,), jnp.float32, math.log(0.3), math.log(3.0)))
    token_scale = jnp.exp(jax.random.uniform(second, (TOKENS,), jnp.float32, math.log(0.3), math.log(3.0)))
    return (base * token_scale[:, None] * feature_scale[None, :]).astype(jnp.float32)


def setup_inputs(seed: int = 0) -> dict:
    key_of = jax.random.split(jax.random.key(seed), 2)
    layer_inputs = draw_layer_inputs(jax.random.fold_in(key_of[1], 71), 0)
    return {"layer_inputs": layer_inputs}


def reference(layer_inputs):
    product = lax.dot_general(layer_inputs, layer_inputs, (((0,), (0,)), ((), ())), precision=lax.Precision.HIGHEST, preferred_element_type=jnp.float32)
    return product / TOKENS
```

```python
import functools

import jax
import jax.numpy as jnp
from jax import lax
from jax.experimental import pallas as pl
from jax.experimental.pallas import tpu as pltpu
from jax.sharding import PartitionSpec as P

MESH = pl.DeviceIdType.MESH
CORES = 2


def bits_of(chips):
    return max(chips.bit_length() - 1, 0)


def chip_at(place, chips):
    total = 0
    for k in range(bits_of(chips)):
        total += 2**k * lax.rem(lax.div(place, 2**k) + lax.div(place, 2 ** (k + 1)), 2)
    return total


def place_of(chip, chips):
    total, above = 0, 0
    for k in reversed(range(bits_of(chips))):
        above = lax.rem(above + lax.rem(lax.div(chip, 2**k), 2), 2)
        total += 2**k * above
    return total


def gather_kernel(
    n_rows, n_cols, x_ref, own_ref, panel_ref,
    all_send, all_recv, up_send, down_send, chain_recv,
    ring_send, ring_recv, twin_send, twin_recv, local_sem,
):
    r, c = lax.axis_index("row"), lax.axis_index("col")
    chips = n_cols // CORES
    chip, core = lax.div(c, CORES), lax.rem(c, CORES)
    twin = c + 1 - 2 * core
    tok = x_ref.shape[0]
    width = own_ref.shape[1]
    half = width // 2
    rows = tok * CORES
    pieces = n_rows * chips
    place, root = place_of(chip, chips), place_of(r, chips)
    is_root = chip == r
    follow = CORES * chip_at(lax.rem(place + 1, chips), chips) + core
    before = CORES * chip_at(lax.rem(place + chips - 1, chips), chips) + core
    ring_to = (follow, before)
    hops = (
        lax.rem(place - root + chips, chips),
        lax.rem(root - place + chips, chips),
    )

    barrier = pltpu.get_barrier_semaphore()

    def greet(k, _):
        pl.semaphore_signal(
            barrier, inc=1, device_id=(r, lax.rem(c + k, n_cols)), device_id_type=MESH
        )
        return 0

    lax.fori_loop(1, n_cols, greet, 0)

    @pl.when(r > 0)
    def _():
        pl.semaphore_signal(barrier, inc=1, device_id=(r - 1, c), device_id_type=MESH)

    @pl.when(r < n_rows - 1)
    def _():
        pl.semaphore_signal(barrier, inc=1, device_id=(r + 1, c), device_id_type=MESH)

    above, below = (r > 0).astype(jnp.int32), (r < n_rows - 1).astype(jnp.int32)
    pl.semaphore_wait(barrier, n_cols - 1 + above + below)

    def token_rows(source):
        return pl.ds(pl.multiple_of((r * n_cols + source) * tok, tok), tok)

    def x_columns(block):
        return pl.ds(pl.multiple_of(block * width, width), width)

    def piece_rows(piece):
        return pl.ds(pl.multiple_of(piece * rows, rows), rows)

    def panel_columns(way, of_core):
        return pl.ds(pl.multiple_of(of_core * width + way * half, half), half)

    def all_copy(k):
        other = lax.rem(c + k, n_cols)
        return pltpu.make_async_remote_copy(
            src_ref=x_ref.at[:, x_columns(other)],
            dst_ref=own_ref.at[token_rows(c)],
            send_sem=all_send.at[other],
            recv_sem=all_recv.at[c],
            device_id=(r, other),
            device_id_type=MESH,
        )

    def chain_copy(piece, step):
        block = own_ref.at[piece_rows(piece)]
        return pltpu.make_async_remote_copy(
            src_ref=block,
            dst_ref=block,
            send_sem=(up_send if step > 0 else down_send).at[piece],
            recv_sem=chain_recv.at[piece],
            device_id=(r + step, c),
            device_id_type=MESH,
        )

    def panel_part(way, piece):
        return panel_ref.at[piece_rows(piece), panel_columns(way, core)]

    def ring_copy(way, piece, from_own):
        source = panel_part(way, piece)
        if from_own:
            source = own_ref.at[piece_rows(piece), pl.ds(way * half, half)]
        return pltpu.make_async_remote_copy(
            src_ref=source,
            dst_ref=panel_part(way, piece),
            send_sem=ring_send.at[way, piece],
            recv_sem=ring_recv.at[way, piece],
            device_id=(r, ring_to[way]),
            device_id_type=MESH,
        )

    def twin_copy(way, piece, from_own):
        source = panel_part(way, piece)
        if from_own:
            source = own_ref.at[piece_rows(piece), pl.ds(way * half, half)]
        return pltpu.make_async_remote_copy(
            src_ref=source,
            dst_ref=panel_part(way, piece),
            send_sem=twin_send.at[way, piece],
            recv_sem=twin_recv.at[way, piece],
            device_id=(r, twin),
            device_id_type=MESH,
        )

    def local_copy(piece):
        return pltpu.make_async_copy(
            own_ref.at[piece_rows(piece)],
            panel_ref.at[piece_rows(piece), pl.ds(pl.multiple_of(core * width, width), width)],
            local_sem.at[piece],
        )

    def own_columns():
        return pltpu.make_async_copy(
            x_ref.at[:, x_columns(c)], own_ref.at[token_rows(c)], all_recv.at[c]
        )

    own_columns().start()

    def send_all(k, _):
        all_copy(k).start()
        return 0

    lax.fori_loop(1, n_cols, send_all, 0)

    def from_root(piece):
        @pl.when(is_root)
        def _():
            for way in range(2):
                if chips > 1:
                    ring_copy(way, piece, True).start()
            for way in range(2):
                twin_copy(way, piece, True).start()
            local_copy(piece).start()

    def own_step(s):
        away, turn = lax.div(s, chips), lax.rem(s, chips)
        group = lax.rem(chip + turn, chips)

        @pl.when(away == 0)
        def _():
            for k in range(CORES):
                source = group * CORES + k
                block = own_ref.at[token_rows(source)]
                pltpu.make_async_copy(block, block, all_recv.at[source]).wait()
            piece = r * chips + group

            @pl.when(r > 0)
            def _():
                chain_copy(piece, -1).start()

            @pl.when(r < n_rows - 1)
            def _():
                chain_copy(piece, 1).start()

            from_root(piece)

        @pl.when(jnp.logical_and(away > 0, r - away >= 0))
        def _():
            piece = (r - away) * chips + group
            chain_copy(piece, 1).wait_recv()

            @pl.when(r < n_rows - 1)
            def _():
                chain_copy(piece, 1).start()

            from_root(piece)

        @pl.when(jnp.logical_and(away > 0, r + away < n_rows))
        def _():
            piece = (r + away) * chips + group
            chain_copy(piece, -1).wait_recv()

            @pl.when(r > 0)
            def _():
                chain_copy(piece, -1).start()

            from_root(piece)

    def pass_on(way, piece):
        ring_copy(way, piece, False).wait_recv()

        @pl.when(hops[way] < chips - 1)
        def _():
            ring_copy(way, piece, False).start()

        twin_copy(way, piece, False).start()

    def ring_step(way, s):
        away, turn = lax.div(s, chips), lax.rem(s, chips)
        group = lax.rem(r + turn, chips)

        @pl.when(r - away >= 0)
        def _():
            pass_on(way, (r - away) * chips + group)

        @pl.when(jnp.logical_and(away > 0, r + away < n_rows))
        def _():
            pass_on(way, (r + away) * chips + group)

    def step(s, _):
        @pl.when(s < pieces)
        def _():
            own_step(s)

        for way in range(2):
            late = s - hops[way]

            @pl.when(
                jnp.logical_and(
                    jnp.logical_not(is_root),
                    jnp.logical_and(late >= 0, late < pieces),
                )
            )
            def _():
                ring_step(way, late)

        return 0

    lax.fori_loop(0, pieces + chips - 1, step, 0)

    def finish_all(k, _):
        all_copy(k).wait_send()
        return 0

    lax.fori_loop(1, n_cols, finish_all, 0)

    def finish(piece, _):
        of_row = lax.div(piece, chips)

        @pl.when(jnp.logical_and(r < n_rows - 1, of_row <= r))
        def _():
            chain_copy(piece, 1).wait_send()

        @pl.when(jnp.logical_and(r > 0, of_row >= r))
        def _():
            chain_copy(piece, -1).wait_send()

        for way in range(2):
            if chips > 1:
                @pl.when(hops[way] < chips - 1)
                def _():
                    ring_copy(way, piece, False).wait_send()

            twin_copy(way, piece, False).wait_send()
            twin_copy(way, piece, False).wait_recv()

        @pl.when(is_root)
        def _():
            local_copy(piece).wait()

        return 0

    lax.fori_loop(0, pieces, finish, 0)


def gather(x, n_rows, n_cols):
    tok, features = x.shape
    width = features // n_cols
    total = tok * n_rows * n_cols
    chips = n_cols // CORES
    pieces = n_rows * chips
    dma = pltpu.SemaphoreType.DMA
    return pl.pallas_call(
        functools.partial(gather_kernel, n_rows, n_cols),
        out_shape=(
            jax.ShapeDtypeStruct((total, width), jnp.float32),
            jax.ShapeDtypeStruct((total, CORES * width), jnp.float32),
        ),
        in_specs=[pl.BlockSpec(memory_space=pl.ANY)],
        out_specs=(pl.BlockSpec(memory_space=pl.ANY),) * 2,
        scratch_shapes=[
            dma((n_cols,)), dma((n_cols,)),
            dma((pieces,)), dma((pieces,)), dma((pieces,)),
            dma((2, pieces)), dma((2, pieces)),
            dma((2, pieces)), dma((2, pieces)),
            dma((pieces,)),
        ],
        compiler_params=pltpu.CompilerParams(collective_id=0, has_side_effects=True),
        name="gather_columns",
    )(x)


def split(x):
    high = x.astype(jnp.bfloat16)
    low = (x - high.astype(jnp.float32)).astype(jnp.bfloat16)
    return high, low


def gram_kernel(scale, panel_ref, own_ref, out_ref, right):
    depth = own_ref.shape[0]

    @pl.when(pl.program_id(0) == 0)
    def _():
        high, low = split(own_ref[...])
        right[pl.ds(0, depth), :] = high
        right[pl.ds(depth, depth), :] = low
        right[pl.ds(2 * depth, depth), :] = high

    high, low = split(panel_ref[...].T)
    left = jnp.concatenate([high, high, low], axis=1)
    product = jnp.dot(left, right[...], preferred_element_type=jnp.float32)
    out_ref[...] = product * scale


def gram(own, panel, tile):
    depth, width = own.shape
    count = panel.shape[1]
    return pl.pallas_call(
        functools.partial(gram_kernel, 1.0 / depth),
        grid=(count // tile,),
        out_shape=jax.ShapeDtypeStruct((count, width), jnp.float32),
        in_specs=[
            pl.BlockSpec((depth, tile), lambda i: (0, i)),
            pl.BlockSpec((depth, width), lambda i: (0, 0), pipeline_mode=pl.Buffered(1)),
        ],
        out_specs=pl.BlockSpec((tile, width), lambda i: (i, 0)),
        scratch_shapes=[pltpu.VMEM((3 * depth, width), jnp.bfloat16)],
        compiler_params=pltpu.CompilerParams(vmem_limit_bytes=56 * 2**20),
        cost_estimate=pl.CostEstimate(
            flops=6 * depth * width * count,
            bytes_accessed=4 * (width * count + depth * (width + count)),
            transcendentals=0,
        ),
        name="gram_blocks",
    )(panel, own)


def shards(x):
    n_rows, n_cols = lax.axis_size("row"), lax.axis_size("col")
    own, panel = gather(x, n_rows, n_cols)
    depth = own.shape[0]
    if depth & (depth - 1):
        raise ValueError("token count")
    return gram(own, panel, 256)


def solution(mesh):
    if mesh.shape["col"] != CORES * mesh.shape["row"]:
        raise ValueError("mesh shape")
    placed = (P(("row", "col"), None),)
    return jax.shard_map(
        shards, mesh=mesh, in_specs=placed, out_specs=P("row", "col"), check_vma=False
    )
```

```python
import functools

import jax
import jax.numpy as jnp
from jax import lax
from jax.experimental import pallas as pl
from jax.experimental.pallas import tpu as pltpu
from jax.sharding import PartitionSpec as P

MESH = pl.DeviceIdType.MESH
CORES = 2
GROUPS = 8
VMEM_LIMIT = 56 * 2**20


def bits_of(chips):
    return max(chips.bit_length() - 1, 0)


def chip_at(place, chips):
    total = 0
    for k in range(bits_of(chips)):
        total += 2**k * lax.rem(lax.div(place, 2**k) + lax.div(place, 2 ** (k + 1)), 2)
    return total


def place_of(chip, chips):
    total, above = 0, 0
    for k in reversed(range(bits_of(chips))):
        above = lax.rem(above + lax.rem(lax.div(chip, 2**k), 2), 2)
        total += 2**k * above
    return total


def gather_kernel(
    n_rows, n_cols, groups, x_ref, own_out, panel_out, own_ref, panel_ref,
    all_send, all_recv, up_send, down_send, chain_recv,
    ring_send, ring_recv, twin_send, twin_recv, local_sem,
):
    r, c = lax.axis_index("row"), lax.axis_index("col")
    chips = n_cols // CORES
    chip, core = lax.div(c, CORES), lax.rem(c, CORES)
    twin = c + 1 - 2 * core
    tok = x_ref.shape[0]
    width = own_ref.shape[1]
    half = width // 2
    per = n_cols // groups
    rows = tok * per
    pieces = n_rows * groups
    place, root = place_of(chip, chips), place_of(r, chips)
    is_root = chip == r
    follow = CORES * chip_at(lax.rem(place + 1, chips), chips) + core
    before = CORES * chip_at(lax.rem(place + chips - 1, chips), chips) + core
    ring_to = (follow, before)
    hops = (
        lax.rem(place - root + chips, chips),
        lax.rem(root - place + chips, chips),
    )

    barrier = pltpu.get_barrier_semaphore()

    def greet(k, _):
        pl.semaphore_signal(
            barrier, inc=1, device_id=(r, lax.rem(c + k, n_cols)), device_id_type=MESH
        )
        return 0

    lax.fori_loop(1, n_cols, greet, 0)

    @pl.when(r > 0)
    def _():
        pl.semaphore_signal(barrier, inc=1, device_id=(r - 1, c), device_id_type=MESH)

    @pl.when(r < n_rows - 1)
    def _():
        pl.semaphore_signal(barrier, inc=1, device_id=(r + 1, c), device_id_type=MESH)

    above, below = (r > 0).astype(jnp.int32), (r < n_rows - 1).astype(jnp.int32)
    pl.semaphore_wait(barrier, n_cols - 1 + above + below)

    def token_rows(source):
        return pl.ds(pl.multiple_of((r * n_cols + source) * tok, tok), tok)

    def x_columns(block):
        return pl.ds(pl.multiple_of(block * width, width), width)

    def piece_rows(piece):
        return pl.ds(pl.multiple_of(piece * rows, rows), rows)

    def panel_columns(way, of_core):
        return pl.ds(pl.multiple_of(of_core * width + way * half, half), half)

    def all_copy(k):
        other = lax.rem(c + k, n_cols)
        return pltpu.make_async_remote_copy(
            src_ref=x_ref.at[:, x_columns(other)],
            dst_ref=own_ref.at[token_rows(c)],
            send_sem=all_send.at[other],
            recv_sem=all_recv.at[c],
            device_id=(r, other),
            device_id_type=MESH,
        )

    def chain_copy(piece, step):
        block = own_ref.at[piece_rows(piece)]
        return pltpu.make_async_remote_copy(
            src_ref=block,
            dst_ref=block,
            send_sem=(up_send if step > 0 else down_send).at[piece],
            recv_sem=chain_recv.at[piece],
            device_id=(r + step, c),
            device_id_type=MESH,
        )

    def panel_part(way, piece):
        return panel_ref.at[piece_rows(piece), panel_columns(way, core)]

    def ring_copy(way, piece, from_own):
        source = panel_part(way, piece)
        if from_own:
            source = own_ref.at[piece_rows(piece), pl.ds(way * half, half)]
        return pltpu.make_async_remote_copy(
            src_ref=source,
            dst_ref=panel_part(way, piece),
            send_sem=ring_send.at[way, piece],
            recv_sem=ring_recv.at[way, piece],
            device_id=(r, ring_to[way]),
            device_id_type=MESH,
        )

    def twin_copy(way, piece, from_own):
        source = panel_part(way, piece)
        if from_own:
            source = own_ref.at[piece_rows(piece), pl.ds(way * half, half)]
        return pltpu.make_async_remote_copy(
            src_ref=source,
            dst_ref=panel_part(way, piece),
            send_sem=twin_send.at[way, piece],
            recv_sem=twin_recv.at[way, piece],
            device_id=(r, twin),
            device_id_type=MESH,
        )

    def local_copy(piece):
        columns = pl.ds(pl.multiple_of(core * width, width), width)
        panel_ref[piece_rows(piece), columns] = own_ref[piece_rows(piece), :]

    def keep_own(piece):
        return pltpu.make_async_copy(
            own_ref.at[piece_rows(piece)],
            own_out.at[piece_rows(piece)],
            local_sem.at[0, piece],
        )

    def keep_panel(piece):
        return pltpu.make_async_copy(
            panel_ref.at[piece_rows(piece)],
            panel_out.at[piece_rows(piece)],
            local_sem.at[1, piece],
        )

    def own_columns():
        return pltpu.make_async_copy(
            x_ref.at[:, x_columns(c)], own_ref.at[token_rows(c)], all_recv.at[c]
        )

    own_columns().start()

    def send_all(k, _):
        all_copy(k).start()
        return 0

    lax.fori_loop(1, n_cols, send_all, 0)

    def from_root(piece):
        keep_own(piece).start()

        @pl.when(is_root)
        def _():
            for way in range(2):
                if chips > 1:
                    ring_copy(way, piece, True).start()
            for way in range(2):
                twin_copy(way, piece, True).start()
            local_copy(piece)

    def own_step(s):
        away, turn = lax.div(s, groups), lax.rem(s, groups)
        group = lax.rem(lax.div(CORES * chip, per) + turn, groups)

        @pl.when(away == 0)
        def _():
            for k in range(per):
                source = group * per + k
                block = own_ref.at[token_rows(source)]
                pltpu.make_async_copy(block, block, all_recv.at[source]).wait()
            piece = r * groups + group

            @pl.when(r > 0)
            def _():
                chain_copy(piece, -1).start()

            @pl.when(r < n_rows - 1)
            def _():
                chain_copy(piece, 1).start()

            from_root(piece)

        @pl.when(jnp.logical_and(away > 0, r - away >= 0))
        def _():
            piece = (r - away) * groups + group
            chain_copy(piece, 1).wait_recv()

            @pl.when(r < n_rows - 1)
            def _():
                chain_copy(piece, 1).start()

            from_root(piece)

        @pl.when(jnp.logical_and(away > 0, r + away < n_rows))
        def _():
            piece = (r + away) * groups + group
            chain_copy(piece, -1).wait_recv()

            @pl.when(r > 0)
            def _():
                chain_copy(piece, -1).start()

            from_root(piece)

    def pass_on(way, piece):
        ring_copy(way, piece, False).wait_recv()

        @pl.when(hops[way] < chips - 1)
        def _():
            ring_copy(way, piece, False).start()

        twin_copy(way, piece, False).start()

    def ring_step(way, s):
        away, turn = lax.div(s, groups), lax.rem(s, groups)
        group = lax.rem(lax.div(CORES * r, per) + turn, groups)

        @pl.when(r - away >= 0)
        def _():
            pass_on(way, (r - away) * groups + group)

        @pl.when(jnp.logical_and(away > 0, r + away < n_rows))
        def _():
            pass_on(way, (r + away) * groups + group)

    def step(s, _):
        @pl.when(s < pieces)
        def _():
            own_step(s)

        for way in range(2):
            late = s - hops[way]

            @pl.when(
                jnp.logical_and(
                    jnp.logical_not(is_root),
                    jnp.logical_and(late >= 0, late < pieces),
                )
            )
            def _():
                ring_step(way, late)

        return 0

    lax.fori_loop(0, pieces + chips - 1, step, 0)

    def finish_all(k, _):
        all_copy(k).wait_send()
        return 0

    lax.fori_loop(1, n_cols, finish_all, 0)

    def finish(piece, _):
        of_row = lax.div(piece, groups)

        @pl.when(jnp.logical_and(r < n_rows - 1, of_row <= r))
        def _():
            chain_copy(piece, 1).wait_send()

        @pl.when(jnp.logical_and(r > 0, of_row >= r))
        def _():
            chain_copy(piece, -1).wait_send()

        for way in range(2):
            if chips > 1:
                @pl.when(hops[way] < chips - 1)
                def _():
                    ring_copy(way, piece, False).wait_send()

            twin_copy(way, piece, False).wait_send()
            twin_copy(way, piece, False).wait_recv()

        keep_panel(piece).start()
        return 0

    lax.fori_loop(0, pieces, finish, 0)

    def finish_kept(piece, _):
        keep_own(piece).wait()
        keep_panel(piece).wait()
        return 0

    lax.fori_loop(0, pieces, finish_kept, 0)


def gather(x, n_rows, n_cols):
    tok, features = x.shape
    width = features // n_cols
    total = tok * n_rows * n_cols
    groups = GROUPS if n_cols % GROUPS == 0 else n_cols
    pieces = n_rows * groups
    dma = pltpu.SemaphoreType.DMA
    return pl.pallas_call(
        functools.partial(gather_kernel, n_rows, n_cols, groups),
        out_shape=(
            jax.ShapeDtypeStruct((total, width), jnp.float32),
            jax.ShapeDtypeStruct((total, CORES * width), jnp.float32),
        ),
        in_specs=[pl.BlockSpec(memory_space=pl.ANY)],
        out_specs=(pl.BlockSpec(memory_space=pl.ANY),) * 2,
        scratch_shapes=[
            pltpu.VMEM((total, width), jnp.float32),
            pltpu.VMEM((total, CORES * width), jnp.float32),
            dma((n_cols,)), dma((n_cols,)),
            dma((pieces,)), dma((pieces,)), dma((pieces,)),
            dma((2, pieces)), dma((2, pieces)),
            dma((2, pieces)), dma((2, pieces)),
            dma((2, pieces)),
        ],
        compiler_params=pltpu.CompilerParams(
            collective_id=0, has_side_effects=True, vmem_limit_bytes=VMEM_LIMIT
        ),
        name="gather_columns",
    )(x)


def split(x):
    high = x.astype(jnp.bfloat16)
    low = (x - high.astype(jnp.float32)).astype(jnp.bfloat16)
    return high, low


def gram_kernel(scale, panel_ref, own_ref, out_ref, right):
    depth = own_ref.shape[0]

    @pl.when(pl.program_id(0) == 0)
    def _():
        high, low = split(own_ref[...])
        right[pl.ds(0, depth), :] = high
        right[pl.ds(depth, depth), :] = low
        right[pl.ds(2 * depth, depth), :] = high

    high, low = split(panel_ref[...].T)
    left = jnp.concatenate([high, high, low], axis=1)
    product = jnp.dot(left, right[...], preferred_element_type=jnp.float32)
    out_ref[...] = product * scale


def gram(own, panel, tile):
    depth, width = own.shape
    count = panel.shape[1]
    return pl.pallas_call(
        functools.partial(gram_kernel, 1.0 / depth),
        grid=(count // tile,),
        out_shape=jax.ShapeDtypeStruct((count, width), jnp.float32),
        in_specs=[
            pl.BlockSpec((depth, tile), lambda i: (0, i)),
            pl.BlockSpec((depth, width), lambda i: (0, 0), pipeline_mode=pl.Buffered(1)),
        ],
        out_specs=pl.BlockSpec((tile, width), lambda i: (i, 0)),
        scratch_shapes=[pltpu.VMEM((3 * depth, width), jnp.bfloat16)],
        compiler_params=pltpu.CompilerParams(vmem_limit_bytes=VMEM_LIMIT),
        cost_estimate=pl.CostEstimate(
            flops=6 * depth * width * count,
            bytes_accessed=4 * (width * count + depth * (width + count)),
            transcendentals=0,
        ),
        name="gram_blocks",
    )(panel, own)


def shards(x):
    n_rows, n_cols = lax.axis_size("row"), lax.axis_size("col")
    own, panel = gather(x, n_rows, n_cols)
    depth = own.shape[0]
    if depth & (depth - 1):
        raise ValueError("token count")
    return gram(own, panel, 512)


def solution(mesh):
    if mesh.shape["col"] != CORES * mesh.shape["row"]:
        raise ValueError("mesh shape")
    placed = (P(("row", "col"), None),)
    return jax.shard_map(
        shards, mesh=mesh, in_specs=placed, out_specs=P("row", "col"), check_vma=False
    )
```

```python
import functools

import jax
import jax.numpy as jnp
from jax import lax
from jax.experimental import pallas as pl
from jax.experimental.pallas import tpu as pltpu
from jax.sharding import PartitionSpec as P

MESH = pl.DeviceIdType.MESH
CORES = 2
GROUPS = 8
LAG = 2
VMEM_LIMIT = 56 * 2**20


def bits_of(chips):
    return max(chips.bit_length() - 1, 0)


def chip_at(place, chips):
    total = 0
    for k in range(bits_of(chips)):
        total += 2**k * lax.rem(lax.div(place, 2**k) + lax.div(place, 2 ** (k + 1)), 2)
    return total


def place_of(chip, chips):
    total, above = 0, 0
    for k in reversed(range(bits_of(chips))):
        above = lax.rem(above + lax.rem(lax.div(chip, 2**k), 2), 2)
        total += 2**k * above
    return total


def gather_kernel(
    n_rows, n_cols, groups, x_ref, own_out, panel_out, own_ref, panel_ref,
    all_send, all_recv, up_send, down_send, chain_recv,
    ring_send, ring_recv, twin_send, twin_recv, local_sem,
):
    r, c = lax.axis_index("row"), lax.axis_index("col")
    chips = n_cols // CORES
    chip, core = lax.div(c, CORES), lax.rem(c, CORES)
    twin = c + 1 - 2 * core
    tok = x_ref.shape[0]
    width = own_ref.shape[1]
    half = width // 2
    per = n_cols // groups
    rows = tok * per
    pieces = n_rows * groups
    place, root = place_of(chip, chips), place_of(r, chips)
    is_root = chip == r
    follow = CORES * chip_at(lax.rem(place + 1, chips), chips) + core
    before = CORES * chip_at(lax.rem(place + chips - 1, chips), chips) + core
    ring_to = (follow, before)
    hops = (
        lax.rem(place - root + chips, chips),
        lax.rem(root - place + chips, chips),
    )

    barrier = pltpu.get_barrier_semaphore()

    def greet(k, _):
        pl.semaphore_signal(
            barrier, inc=1, device_id=(r, lax.rem(c + k, n_cols)), device_id_type=MESH
        )
        return 0

    lax.fori_loop(1, n_cols, greet, 0)

    @pl.when(r > 0)
    def _():
        pl.semaphore_signal(barrier, inc=1, device_id=(r - 1, c), device_id_type=MESH)

    @pl.when(r < n_rows - 1)
    def _():
        pl.semaphore_signal(barrier, inc=1, device_id=(r + 1, c), device_id_type=MESH)

    above, below = (r > 0).astype(jnp.int32), (r < n_rows - 1).astype(jnp.int32)
    pl.semaphore_wait(barrier, n_cols - 1 + above + below)

    def token_rows(source):
        return pl.ds(pl.multiple_of((r * n_cols + source) * tok, tok), tok)

    def x_columns(block):
        return pl.ds(pl.multiple_of(block * width, width), width)

    def piece_rows(piece):
        return pl.ds(pl.multiple_of(piece * rows, rows), rows)

    def panel_columns(way, of_core):
        return pl.ds(pl.multiple_of(of_core * width + way * half, half), half)

    def all_copy(k):
        other = lax.rem(c + k, n_cols)
        return pltpu.make_async_remote_copy(
            src_ref=x_ref.at[:, x_columns(other)],
            dst_ref=own_ref.at[token_rows(c)],
            send_sem=all_send,
            recv_sem=all_recv.at[c],
            device_id=(r, other),
            device_id_type=MESH,
        )

    def chain_copy(piece, step):
        block = own_ref.at[piece_rows(piece)]
        return pltpu.make_async_remote_copy(
            src_ref=block,
            dst_ref=block,
            send_sem=(up_send if step > 0 else down_send).at[lax.div(piece, groups)],
            recv_sem=chain_recv.at[piece],
            device_id=(r + step, c),
            device_id_type=MESH,
        )

    def panel_part(way, piece):
        return panel_ref.at[piece_rows(piece), panel_columns(way, core)]

    def ring_copy(way, piece, from_own):
        source = panel_part(way, piece)
        if from_own:
            source = own_ref.at[piece_rows(piece), pl.ds(way * half, half)]
        return pltpu.make_async_remote_copy(
            src_ref=source,
            dst_ref=panel_part(way, piece),
            send_sem=ring_send.at[way],
            recv_sem=ring_recv.at[way, piece],
            device_id=(r, ring_to[way]),
            device_id_type=MESH,
        )

    def twin_copy(way, piece, from_own):
        source = panel_part(way, piece)
        if from_own:
            source = own_ref.at[piece_rows(piece), pl.ds(way * half, half)]
        return pltpu.make_async_remote_copy(
            src_ref=source,
            dst_ref=panel_part(way, piece),
            send_sem=twin_send,
            recv_sem=twin_recv.at[piece],
            device_id=(r, twin),
            device_id_type=MESH,
        )

    def local_copy(piece):
        columns = pl.ds(pl.multiple_of(core * width, width), width)
        panel_ref[piece_rows(piece), columns] = own_ref[piece_rows(piece), :]

    def keep_own(piece):
        return pltpu.make_async_copy(
            own_ref.at[piece_rows(piece)],
            own_out.at[piece_rows(piece)],
            local_sem.at[0],
        )

    def keep_panel(piece):
        return pltpu.make_async_copy(
            panel_ref.at[piece_rows(piece)],
            panel_out.at[piece_rows(piece)],
            local_sem.at[1],
        )

    def own_columns():
        return pltpu.make_async_copy(
            x_ref.at[:, x_columns(c)], own_ref.at[token_rows(c)], all_recv.at[c]
        )

    own_columns().start()

    def send_all(k, _):
        all_copy(k).start()
        return 0

    lax.fori_loop(1, n_cols, send_all, 0)

    def from_root(piece):
        keep_own(piece).start()

        @pl.when(is_root)
        def _():
            for way in range(2):
                if chips > 1:
                    ring_copy(way, piece, True).start()
            for way in range(2):
                twin_copy(way, piece, True).start()
            local_copy(piece)

    def own_step(s):
        away, turn = lax.div(s, groups), lax.rem(s, groups)
        group = lax.rem(lax.div(CORES * chip, per) + turn, groups)

        @pl.when(away == 0)
        def _():
            for k in range(per):
                source = group * per + k
                block = own_ref.at[token_rows(source)]
                pltpu.make_async_copy(block, block, all_recv.at[source]).wait()
            piece = r * groups + group

            @pl.when(r > 0)
            def _():
                chain_copy(piece, -1).start()

            @pl.when(r < n_rows - 1)
            def _():
                chain_copy(piece, 1).start()

            from_root(piece)

        @pl.when(jnp.logical_and(away > 0, r - away >= 0))
        def _():
            piece = (r - away) * groups + group
            chain_copy(piece, 1).wait_recv()

            @pl.when(r < n_rows - 1)
            def _():
                chain_copy(piece, 1).start()

            from_root(piece)

        @pl.when(jnp.logical_and(away > 0, r + away < n_rows))
        def _():
            piece = (r + away) * groups + group
            chain_copy(piece, -1).wait_recv()

            @pl.when(r > 0)
            def _():
                chain_copy(piece, -1).start()

            from_root(piece)

    def pass_on(way, piece):
        ring_copy(way, piece, False).wait_recv()

        @pl.when(hops[way] < chips - 1)
        def _():
            ring_copy(way, piece, False).start()

        twin_copy(way, piece, False).start()

    def ring_step(way, s):
        away, turn = lax.div(s, groups), lax.rem(s, groups)
        group = lax.rem(lax.div(CORES * r, per) + turn, groups)

        @pl.when(r - away >= 0)
        def _():
            pass_on(way, (r - away) * groups + group)

        @pl.when(jnp.logical_and(away > 0, r + away < n_rows))
        def _():
            pass_on(way, (r + away) * groups + group)

    def keep(piece):
        columns = pl.ds(pl.multiple_of((1 - core) * width, width), width)
        part = panel_ref.at[piece_rows(piece), columns]
        pltpu.make_async_copy(part, part, twin_recv.at[piece]).wait()
        keep_panel(piece).start()

    def keep_step(s):
        away, turn = lax.div(s, groups), lax.rem(s, groups)
        group = lax.rem(lax.div(CORES * r, per) + turn, groups)

        @pl.when(r - away >= 0)
        def _():
            keep((r - away) * groups + group)

        @pl.when(jnp.logical_and(away > 0, r + away < n_rows))
        def _():
            keep((r + away) * groups + group)

    def step(s, _):
        @pl.when(s < pieces)
        def _():
            own_step(s)

        for way in range(2):
            late = s - LAG * hops[way]

            @pl.when(
                jnp.logical_and(
                    jnp.logical_not(is_root),
                    jnp.logical_and(late >= 0, late < pieces),
                )
            )
            def _():
                ring_step(way, late)

        last = s - LAG * chips

        @pl.when(last >= 0)
        def _():
            keep_step(last)

        return 0

    lax.fori_loop(0, pieces + LAG * chips, step, 0)

    def drain(ref, sem):
        pltpu.make_async_copy(ref, ref, sem).wait()

    drain(own_ref.at[pl.ds(0, (n_cols - 1) * tok)], all_send)
    drain(own_ref, twin_send)
    drain(own_ref, local_sem.at[0])
    drain(panel_ref, local_sem.at[1])
    for way in range(2):
        if chips > 1:
            @pl.when(hops[way] < chips - 1)
            def _():
                drain(own_ref.at[:, pl.ds(0, half)], ring_send.at[way])

    for block in range(n_rows):
        sent = own_ref.at[pl.ds(block * n_cols * tok, n_cols * tok)]

        @pl.when(jnp.logical_and(r < n_rows - 1, block <= r))
        def _():
            drain(sent, up_send.at[block])

        @pl.when(jnp.logical_and(r > 0, block >= r))
        def _():
            drain(sent, down_send.at[block])


def gather(x, n_rows, n_cols):
    tok, features = x.shape
    width = features // n_cols
    total = tok * n_rows * n_cols
    groups = GROUPS if n_cols % GROUPS == 0 else n_cols
    pieces = n_rows * groups
    dma = pltpu.SemaphoreType.DMA
    return pl.pallas_call(
        functools.partial(gather_kernel, n_rows, n_cols, groups),
        out_shape=(
            jax.ShapeDtypeStruct((total, width), jnp.float32),
            jax.ShapeDtypeStruct((total, CORES * width), jnp.float32),
        ),
        in_specs=[pl.BlockSpec(memory_space=pl.ANY)],
        out_specs=(pl.BlockSpec(memory_space=pl.ANY),) * 2,
        scratch_shapes=[
            pltpu.VMEM((total, width), jnp.float32),
            pltpu.VMEM((total, CORES * width), jnp.float32),
            dma, dma((n_cols,)),
            dma((n_rows,)), dma((n_rows,)), dma((pieces,)),
            dma((2,)), dma((2, pieces)),
            dma, dma((pieces,)),
            dma((2,)),
        ],
        compiler_params=pltpu.CompilerParams(
            collective_id=0, has_side_effects=True, vmem_limit_bytes=VMEM_LIMIT
        ),
        name="gather_columns",
    )(x)


def split(x):
    high = x.astype(jnp.bfloat16)
    low = (x - high.astype(jnp.float32)).astype(jnp.bfloat16)
    return high, low


def gram_kernel(scale, panel_ref, own_ref, out_ref, right):
    depth = own_ref.shape[0]

    @pl.when(pl.program_id(0) == 0)
    def _():
        high, low = split(own_ref[...])
        right[pl.ds(0, depth), :] = high
        right[pl.ds(depth, depth), :] = low
        right[pl.ds(2 * depth, depth), :] = high

    high, low = split(panel_ref[...].T)
    left = jnp.concatenate([high, high, low], axis=1)
    product = jnp.dot(left, right[...], preferred_element_type=jnp.float32)
    out_ref[...] = product * scale


def gram(own, panel, tile):
    depth, width = own.shape
    count = panel.shape[1]
    return pl.pallas_call(
        functools.partial(gram_kernel, 1.0 / depth),
        grid=(count // tile,),
        out_shape=jax.ShapeDtypeStruct((count, width), jnp.float32),
        in_specs=[
            pl.BlockSpec((depth, tile), lambda i: (0, i)),
            pl.BlockSpec((depth, width), lambda i: (0, 0), pipeline_mode=pl.Buffered(1)),
        ],
        out_specs=pl.BlockSpec((tile, width), lambda i: (i, 0)),
        scratch_shapes=[pltpu.VMEM((3 * depth, width), jnp.bfloat16)],
        compiler_params=pltpu.CompilerParams(vmem_limit_bytes=VMEM_LIMIT),
        cost_estimate=pl.CostEstimate(
            flops=6 * depth * width * count,
            bytes_accessed=4 * (width * count + depth * (width + count)),
            transcendentals=0,
        ),
        name="gram_blocks",
    )(panel, own)


def shards(x):
    n_rows, n_cols = lax.axis_size("row"), lax.axis_size("col")
    own, panel = gather(x, n_rows, n_cols)
    depth = own.shape[0]
    if depth & (depth - 1):
        raise ValueError("token count")
    return gram(own, panel, 512)


def solution(mesh):
    if mesh.shape["col"] != CORES * mesh.shape["row"]:
        raise ValueError("mesh shape")
    placed = (P(("row", "col"), None),)
    return jax.shard_map(
        shards, mesh=mesh, in_specs=placed, out_specs=P("row", "col"), check_vma=False
    )
```

```python
import functools

import jax
import jax.numpy as jnp
from jax import lax
from jax.experimental import pallas as pl
from jax.experimental.pallas import tpu as pltpu
from jax.sharding import PartitionSpec as P

MESH = pl.DeviceIdType.MESH
CORES = 2
GROUPS = 8
LAG = 2
TILE = 512
VMEM_LIMIT = 56 * 2**20


def bits_of(chips):
    return max(chips.bit_length() - 1, 0)


def chip_at(place, chips):
    total = 0
    for k in range(bits_of(chips)):
        total += 2**k * lax.rem(lax.div(place, 2**k) + lax.div(place, 2 ** (k + 1)), 2)
    return total


def place_of(chip, chips):
    total, above = 0, 0
    for k in reversed(range(bits_of(chips))):
        above = lax.rem(above + lax.rem(lax.div(chip, 2**k), 2), 2)
        total += 2**k * above
    return total


def split(x):
    high = x.astype(jnp.bfloat16)
    low = (x - high.astype(jnp.float32)).astype(jnp.bfloat16)
    return high, low


def gather_kernel(
    n_rows, n_cols, groups, x_ref, own_out, panel_out, cross_out,
    own_ref, panel_ref, right_ref, cross_ref, cross_sem,
    all_send, all_recv, up_send, down_send, chain_recv,
    ring_send, ring_recv, twin_send, twin_recv, local_sem,
):
    r, c = lax.axis_index("row"), lax.axis_index("col")
    chips = n_cols // CORES
    chip, core = lax.div(c, CORES), lax.rem(c, CORES)
    twin = c + 1 - 2 * core
    tok = x_ref.shape[0]
    width = own_ref.shape[1]
    half = width // 2
    per = n_cols // groups
    rows = tok * per
    pieces = n_rows * groups
    place, root = place_of(chip, chips), place_of(r, chips)
    is_root = chip == r
    follow = CORES * chip_at(lax.rem(place + 1, chips), chips) + core
    before = CORES * chip_at(lax.rem(place + chips - 1, chips), chips) + core
    ring_to = (follow, before)
    hops = (
        lax.rem(place - root + chips, chips),
        lax.rem(root - place + chips, chips),
    )

    barrier = pltpu.get_barrier_semaphore()

    def greet(k, _):
        pl.semaphore_signal(
            barrier, inc=1, device_id=(r, lax.rem(c + k, n_cols)), device_id_type=MESH
        )
        return 0

    lax.fori_loop(1, n_cols, greet, 0)

    @pl.when(r > 0)
    def _():
        pl.semaphore_signal(barrier, inc=1, device_id=(r - 1, c), device_id_type=MESH)

    @pl.when(r < n_rows - 1)
    def _():
        pl.semaphore_signal(barrier, inc=1, device_id=(r + 1, c), device_id_type=MESH)

    above, below = (r > 0).astype(jnp.int32), (r < n_rows - 1).astype(jnp.int32)
    pl.semaphore_wait(barrier, n_cols - 1 + above + below)

    def token_rows(source):
        return pl.ds(pl.multiple_of((r * n_cols + source) * tok, tok), tok)

    def x_columns(block):
        return pl.ds(pl.multiple_of(block * width, width), width)

    def piece_rows(piece):
        return pl.ds(pl.multiple_of(piece * rows, rows), rows)

    def panel_columns(way, of_core):
        return pl.ds(pl.multiple_of(of_core * width + way * half, half), half)

    def all_copy(k):
        other = lax.rem(c + k, n_cols)
        return pltpu.make_async_remote_copy(
            src_ref=x_ref.at[:, x_columns(other)],
            dst_ref=own_ref.at[token_rows(c)],
            send_sem=all_send,
            recv_sem=all_recv.at[c],
            device_id=(r, other),
            device_id_type=MESH,
        )

    def chain_copy(piece, step):
        block = own_ref.at[piece_rows(piece)]
        return pltpu.make_async_remote_copy(
            src_ref=block,
            dst_ref=block,
            send_sem=(up_send if step > 0 else down_send).at[lax.div(piece, groups)],
            recv_sem=chain_recv.at[piece],
            device_id=(r + step, c),
            device_id_type=MESH,
        )

    def panel_part(way, piece):
        return panel_ref.at[piece_rows(piece), panel_columns(way, core)]

    def ring_copy(way, piece, from_own):
        source = panel_part(way, piece)
        if from_own:
            source = own_ref.at[piece_rows(piece), pl.ds(way * half, half)]
        return pltpu.make_async_remote_copy(
            src_ref=source,
            dst_ref=panel_part(way, piece),
            send_sem=ring_send.at[way],
            recv_sem=ring_recv.at[way, piece],
            device_id=(r, ring_to[way]),
            device_id_type=MESH,
        )

    def twin_copy(way, piece, from_own):
        source = panel_part(way, piece)
        if from_own:
            source = own_ref.at[piece_rows(piece), pl.ds(way * half, half)]
        return pltpu.make_async_remote_copy(
            src_ref=source,
            dst_ref=panel_part(way, piece),
            send_sem=twin_send,
            recv_sem=twin_recv.at[piece],
            device_id=(r, twin),
            device_id_type=MESH,
        )

    def local_copy(piece):
        columns = pl.ds(pl.multiple_of(core * width, width), width)
        panel_ref[piece_rows(piece), columns] = own_ref[piece_rows(piece), :]

    def keep_own(piece):
        return pltpu.make_async_copy(
            own_ref.at[piece_rows(piece)],
            own_out.at[piece_rows(piece)],
            local_sem.at[0],
        )

    def keep_panel(piece):
        return pltpu.make_async_copy(
            panel_ref.at[piece_rows(piece)],
            panel_out.at[piece_rows(piece)],
            local_sem.at[1],
        )

    def own_columns():
        return pltpu.make_async_copy(
            x_ref.at[:, x_columns(c)], own_ref.at[token_rows(c)], all_recv.at[c]
        )

    own_columns().start()

    def send_all(k, _):
        all_copy(k).start()
        return 0

    lax.fori_loop(1, n_cols, send_all, 0)

    def from_root(piece):
        keep_own(piece).start()

        @pl.when(is_root)
        def _():
            for way in range(2):
                if chips > 1:
                    ring_copy(way, piece, True).start()
            for way in range(2):
                twin_copy(way, piece, True).start()
            local_copy(piece)

    def own_step(s):
        away, turn = lax.div(s, groups), lax.rem(s, groups)
        group = lax.rem(lax.div(CORES * chip, per) + turn, groups)

        @pl.when(away == 0)
        def _():
            for k in range(per):
                source = group * per + k
                block = own_ref.at[token_rows(source)]
                pltpu.make_async_copy(block, block, all_recv.at[source]).wait()
            piece = r * groups + group

            @pl.when(r > 0)
            def _():
                chain_copy(piece, -1).start()

            @pl.when(r < n_rows - 1)
            def _():
                chain_copy(piece, 1).start()

            from_root(piece)

        @pl.when(jnp.logical_and(away > 0, r - away >= 0))
        def _():
            piece = (r - away) * groups + group
            chain_copy(piece, 1).wait_recv()

            @pl.when(r < n_rows - 1)
            def _():
                chain_copy(piece, 1).start()

            from_root(piece)

        @pl.when(jnp.logical_and(away > 0, r + away < n_rows))
        def _():
            piece = (r + away) * groups + group
            chain_copy(piece, -1).wait_recv()

            @pl.when(r > 0)
            def _():
                chain_copy(piece, -1).start()

            from_root(piece)

    def pass_on(way, piece):
        ring_copy(way, piece, False).wait_recv()

        @pl.when(hops[way] < chips - 1)
        def _():
            ring_copy(way, piece, False).start()

        twin_copy(way, piece, False).start()

    def ring_step(way, s):
        away, turn = lax.div(s, groups), lax.rem(s, groups)
        group = lax.rem(lax.div(CORES * r, per) + turn, groups)

        @pl.when(r - away >= 0)
        def _():
            pass_on(way, (r - away) * groups + group)

        @pl.when(jnp.logical_and(away > 0, r + away < n_rows))
        def _():
            pass_on(way, (r + away) * groups + group)

    def keep(piece):
        columns = pl.ds(pl.multiple_of((1 - core) * width, width), width)
        part = panel_ref.at[piece_rows(piece), columns]
        pltpu.make_async_copy(part, part, twin_recv.at[piece]).wait()
        keep_panel(piece).start()

    def keep_step(s):
        away, turn = lax.div(s, groups), lax.rem(s, groups)
        group = lax.rem(lax.div(CORES * r, per) + turn, groups)

        @pl.when(r - away >= 0)
        def _():
            keep((r - away) * groups + group)

        @pl.when(jnp.logical_and(away > 0, r + away < n_rows))
        def _():
            keep((r + away) * groups + group)

    tiles = panel_ref.shape[1] // TILE
    early = n_rows // 2 * groups + LAG * chips
    near_depth = own_ref.shape[0] // 2
    near = pl.ds(pl.multiple_of(lax.div(r, n_rows // 2) * near_depth, near_depth), near_depth)

    def cross_copy(tile):
        slot = lax.rem(tile, 2)
        return pltpu.make_async_copy(
            cross_ref.at[slot],
            cross_out.at[pl.ds(pl.multiple_of(tile * TILE, TILE), TILE)],
            cross_sem.at[slot],
        )

    def step(s, _):
        @pl.when(s < pieces)
        def _():
            own_step(s)

        for way in range(2):
            late = s - LAG * hops[way]

            @pl.when(
                jnp.logical_and(
                    jnp.logical_not(is_root),
                    jnp.logical_and(late >= 0, late < pieces),
                )
            )
            def _():
                ring_step(way, late)

        last = s - LAG * chips

        @pl.when(last >= 0)
        def _():
            keep_step(last)

        tile = s - early

        @pl.when(tile == 0)
        def _():
            high, low = split(own_ref[near, :])
            right_ref[pl.ds(0, near_depth), :] = low
            right_ref[pl.ds(near_depth, near_depth), :] = high

        @pl.when(jnp.logical_and(tile >= 0, tile < tiles))
        def _():
            slot = lax.rem(tile, 2)

            @pl.when(tile >= 2)
            def _():
                cross_copy(tile - 2).wait()

            columns = pl.ds(pl.multiple_of(tile * TILE, TILE), TILE)
            high, low = split(panel_ref[near, columns].T)
            left = jnp.concatenate([high, low], axis=1)
            cross = jnp.dot(left, right_ref[...], preferred_element_type=jnp.float32)
            cross_ref[slot] = cross.astype(jnp.bfloat16)
            cross_copy(tile).start()

        return 0

    lax.fori_loop(0, early + max(tiles, pieces + LAG * chips - early), step, 0)
    for tile in range(max(tiles - 2, 0), tiles):
        cross_copy(tile).wait()

    def drain(ref, sem):
        pltpu.make_async_copy(ref, ref, sem).wait()

    drain(own_ref.at[pl.ds(0, (n_cols - 1) * tok)], all_send)
    drain(own_ref, twin_send)
    drain(own_ref, local_sem.at[0])
    drain(panel_ref, local_sem.at[1])
    for way in range(2):
        if chips > 1:
            @pl.when(hops[way] < chips - 1)
            def _():
                drain(own_ref.at[:, pl.ds(0, half)], ring_send.at[way])

    for block in range(n_rows):
        sent = own_ref.at[pl.ds(block * n_cols * tok, n_cols * tok)]

        @pl.when(jnp.logical_and(r < n_rows - 1, block <= r))
        def _():
            drain(sent, up_send.at[block])

        @pl.when(jnp.logical_and(r > 0, block >= r))
        def _():
            drain(sent, down_send.at[block])


def gather(x, n_rows, n_cols):
    tok, features = x.shape
    width = features // n_cols
    total = tok * n_rows * n_cols
    groups = GROUPS if n_cols % GROUPS == 0 else n_cols
    pieces = n_rows * groups
    dma = pltpu.SemaphoreType.DMA
    return pl.pallas_call(
        functools.partial(gather_kernel, n_rows, n_cols, groups),
        out_shape=(
            jax.ShapeDtypeStruct((total, width), jnp.float32),
            jax.ShapeDtypeStruct((total, CORES * width), jnp.float32),
            jax.ShapeDtypeStruct((CORES * width, width), jnp.bfloat16),
        ),
        in_specs=[pl.BlockSpec(memory_space=pl.ANY)],
        out_specs=(pl.BlockSpec(memory_space=pl.ANY),) * 3,
        scratch_shapes=[
            pltpu.VMEM((total, width), jnp.float32),
            pltpu.VMEM((total, CORES * width), jnp.float32),
            pltpu.VMEM((total, width), jnp.bfloat16),
            pltpu.VMEM((2, TILE, width), jnp.bfloat16),
            dma((2,)),
            dma, dma((n_cols,)),
            dma((n_rows,)), dma((n_rows,)), dma((pieces,)),
            dma((2,)), dma((2, pieces)),
            dma, dma((pieces,)),
            dma((2,)),
        ],
        compiler_params=pltpu.CompilerParams(
            collective_id=0, has_side_effects=True, vmem_limit_bytes=VMEM_LIMIT
        ),
        name="gather_columns",
    )(x)


def gram_kernel(n_rows, scale, panel_ref, own_ref, cross_ref, out_ref, right):
    depth = own_ref.shape[0]
    half = depth // 2
    side = 1 - lax.div(lax.axis_index("row"), n_rows // 2)
    far = pl.ds(pl.multiple_of(side * half, half), half)

    @pl.when(pl.program_id(0) == 0)
    def _():
        right[pl.ds(0, depth), :] = own_ref[...].astype(jnp.bfloat16)
        high, low = split(own_ref[far, :])
        right[pl.ds(depth, half), :] = low
        right[pl.ds(depth + half, half), :] = high

    high, low = split(panel_ref[far, :].T)
    left = jnp.concatenate([panel_ref[...].T.astype(jnp.bfloat16), high, low], axis=1)
    product = jnp.dot(left, right[...], preferred_element_type=jnp.float32)
    out_ref[...] = (product + cross_ref[...].astype(jnp.float32)) * scale


def gram(own, panel, cross, n_rows):
    depth, width = own.shape
    count = panel.shape[1]
    return pl.pallas_call(
        functools.partial(gram_kernel, n_rows, 1.0 / depth),
        grid=(count // TILE,),
        out_shape=jax.ShapeDtypeStruct((count, width), jnp.float32),
        in_specs=[
            pl.BlockSpec((depth, TILE), lambda i: (0, i)),
            pl.BlockSpec((depth, width), lambda i: (0, 0), pipeline_mode=pl.Buffered(1)),
            pl.BlockSpec((TILE, width), lambda i: (i, 0)),
        ],
        out_specs=pl.BlockSpec((TILE, width), lambda i: (i, 0)),
        scratch_shapes=[pltpu.VMEM((2 * depth, width), jnp.bfloat16)],
        compiler_params=pltpu.CompilerParams(vmem_limit_bytes=VMEM_LIMIT),
        cost_estimate=pl.CostEstimate(
            flops=4 * depth * width * count,
            bytes_accessed=4 * (width * count + depth * (width + count)) + 2 * width * count,
            transcendentals=0,
        ),
        name="gram_blocks",
    )(panel, own, cross)


def shards(x):
    n_rows, n_cols = lax.axis_size("row"), lax.axis_size("col")
    own, panel, cross = gather(x, n_rows, n_cols)
    depth = own.shape[0]
    if depth & (depth - 1):
        raise ValueError("token count")
    return gram(own, panel, cross, n_rows)


def solution(mesh):
    if mesh.shape["col"] != CORES * mesh.shape["row"]:
        raise ValueError("mesh shape")
    placed = (P(("row", "col"), None),)
    return jax.shard_map(
        shards, mesh=mesh, in_specs=placed, out_specs=P("row", "col"), check_vma=False
    )
```

```python
import functools

import jax
import jax.numpy as jnp
from jax import lax
from jax.experimental import pallas as pl
from jax.experimental.pallas import tpu as pltpu
from jax.sharding import PartitionSpec as P

MESH = pl.DeviceIdType.MESH
CORES = 2
GROUPS = 8
LAG = 2
TILE = 512
VMEM_LIMIT = 56 * 2**20


def bits_of(chips):
    return max(chips.bit_length() - 1, 0)


def chip_at(place, chips):
    total = 0
    for k in range(bits_of(chips)):
        total += 2**k * lax.rem(lax.div(place, 2**k) + lax.div(place, 2 ** (k + 1)), 2)
    return total


def place_of(chip, chips):
    total, above = 0, 0
    for k in reversed(range(bits_of(chips))):
        above = lax.rem(above + lax.rem(lax.div(chip, 2**k), 2), 2)
        total += 2**k * above
    return total


def split(x):
    high = x.astype(jnp.bfloat16)
    low = (x - high.astype(jnp.float32)).astype(jnp.bfloat16)
    return high, low


def gather_kernel(
    n_rows, n_cols, groups, x_ref, own_out, panel_out, cross_out, near_out, left_out,
    own_ref, panel_ref, right_ref, cross_ref, left_ref, cross_sem, left_sem, near_sem,
    all_send, all_recv, up_send, down_send, chain_recv,
    ring_send, ring_recv, twin_send, twin_recv, local_sem,
):
    r, c = lax.axis_index("row"), lax.axis_index("col")
    chips = n_cols // CORES
    chip, core = lax.div(c, CORES), lax.rem(c, CORES)
    twin = c + 1 - 2 * core
    tok = x_ref.shape[0]
    width = own_ref.shape[1]
    half = width // 2
    per = n_cols // groups
    rows = tok * per
    pieces = n_rows * groups
    place, root = place_of(chip, chips), place_of(r, chips)
    is_root = chip == r
    follow = CORES * chip_at(lax.rem(place + 1, chips), chips) + core
    before = CORES * chip_at(lax.rem(place + chips - 1, chips), chips) + core
    ring_to = (follow, before)
    hops = (
        lax.rem(place - root + chips, chips),
        lax.rem(root - place + chips, chips),
    )

    barrier = pltpu.get_barrier_semaphore()

    def greet(k, _):
        pl.semaphore_signal(
            barrier, inc=1, device_id=(r, lax.rem(c + k, n_cols)), device_id_type=MESH
        )
        return 0

    lax.fori_loop(1, n_cols, greet, 0)

    @pl.when(r > 0)
    def _():
        pl.semaphore_signal(barrier, inc=1, device_id=(r - 1, c), device_id_type=MESH)

    @pl.when(r < n_rows - 1)
    def _():
        pl.semaphore_signal(barrier, inc=1, device_id=(r + 1, c), device_id_type=MESH)

    above, below = (r > 0).astype(jnp.int32), (r < n_rows - 1).astype(jnp.int32)
    pl.semaphore_wait(barrier, n_cols - 1 + above + below)

    def token_rows(source):
        return pl.ds(pl.multiple_of((r * n_cols + source) * tok, tok), tok)

    def x_columns(block):
        return pl.ds(pl.multiple_of(block * width, width), width)

    def piece_rows(piece):
        return pl.ds(pl.multiple_of(piece * rows, rows), rows)

    def panel_columns(way, of_core):
        return pl.ds(pl.multiple_of(of_core * width + way * half, half), half)

    def all_copy(k):
        other = lax.rem(c + k, n_cols)
        return pltpu.make_async_remote_copy(
            src_ref=x_ref.at[:, x_columns(other)],
            dst_ref=own_ref.at[token_rows(c)],
            send_sem=all_send,
            recv_sem=all_recv.at[c],
            device_id=(r, other),
            device_id_type=MESH,
        )

    def chain_copy(piece, step):
        block = own_ref.at[piece_rows(piece)]
        return pltpu.make_async_remote_copy(
            src_ref=block,
            dst_ref=block,
            send_sem=(up_send if step > 0 else down_send).at[lax.div(piece, groups)],
            recv_sem=chain_recv.at[piece],
            device_id=(r + step, c),
            device_id_type=MESH,
        )

    def panel_part(way, piece):
        return panel_ref.at[piece_rows(piece), panel_columns(way, core)]

    def ring_copy(way, piece, from_own):
        source = panel_part(way, piece)
        if from_own:
            source = own_ref.at[piece_rows(piece), pl.ds(way * half, half)]
        return pltpu.make_async_remote_copy(
            src_ref=source,
            dst_ref=panel_part(way, piece),
            send_sem=ring_send.at[way],
            recv_sem=ring_recv.at[way, piece],
            device_id=(r, ring_to[way]),
            device_id_type=MESH,
        )

    def twin_copy(way, piece, from_own):
        source = panel_part(way, piece)
        if from_own:
            source = own_ref.at[piece_rows(piece), pl.ds(way * half, half)]
        return pltpu.make_async_remote_copy(
            src_ref=source,
            dst_ref=panel_part(way, piece),
            send_sem=twin_send,
            recv_sem=twin_recv.at[piece],
            device_id=(r, twin),
            device_id_type=MESH,
        )

    def local_copy(piece):
        columns = pl.ds(pl.multiple_of(core * width, width), width)
        panel_ref[piece_rows(piece), columns] = own_ref[piece_rows(piece), :]

    near_depth = own_ref.shape[0] // 2
    near_side = lax.div(r, n_rows // 2)
    far_side = 1 - near_side
    near = pl.ds(pl.multiple_of(near_side * near_depth, near_depth), near_depth)

    def is_far(piece):
        return lax.div(piece, pieces // 2) == far_side

    def far_rows(piece):
        return piece_rows(piece - far_side * (pieces // 2))

    def keep_own(piece):
        return pltpu.make_async_copy(
            own_ref.at[piece_rows(piece)],
            own_out.at[far_rows(piece)],
            local_sem.at[0],
        )

    def keep_panel(piece):
        return pltpu.make_async_copy(
            panel_ref.at[piece_rows(piece)],
            panel_out.at[far_rows(piece)],
            local_sem.at[1],
        )

    def near_copy():
        return pltpu.make_async_copy(
            right_ref.at[pl.ds(near_depth, near_depth)], near_out, near_sem
        )

    def own_columns():
        return pltpu.make_async_copy(
            x_ref.at[:, x_columns(c)], own_ref.at[token_rows(c)], all_recv.at[c]
        )

    own_columns().start()

    def send_all(k, _):
        all_copy(k).start()
        return 0

    lax.fori_loop(1, n_cols, send_all, 0)

    def from_root(piece):
        @pl.when(is_far(piece))
        def _():
            keep_own(piece).start()

        @pl.when(is_root)
        def _():
            for way in range(2):
                if chips > 1:
                    ring_copy(way, piece, True).start()
            for way in range(2):
                twin_copy(way, piece, True).start()
            local_copy(piece)

    def own_step(s):
        away, turn = lax.div(s, groups), lax.rem(s, groups)
        group = lax.rem(lax.div(CORES * chip, per) + turn, groups)

        @pl.when(away == 0)
        def _():
            for k in range(per):
                source = group * per + k
                block = own_ref.at[token_rows(source)]
                pltpu.make_async_copy(block, block, all_recv.at[source]).wait()
            piece = r * groups + group

            @pl.when(r > 0)
            def _():
                chain_copy(piece, -1).start()

            @pl.when(r < n_rows - 1)
            def _():
                chain_copy(piece, 1).start()

            from_root(piece)

        @pl.when(jnp.logical_and(away > 0, r - away >= 0))
        def _():
            piece = (r - away) * groups + group
            chain_copy(piece, 1).wait_recv()

            @pl.when(r < n_rows - 1)
            def _():
                chain_copy(piece, 1).start()

            from_root(piece)

        @pl.when(jnp.logical_and(away > 0, r + away < n_rows))
        def _():
            piece = (r + away) * groups + group
            chain_copy(piece, -1).wait_recv()

            @pl.when(r > 0)
            def _():
                chain_copy(piece, -1).start()

            from_root(piece)

    def pass_on(way, piece):
        ring_copy(way, piece, False).wait_recv()

        @pl.when(hops[way] < chips - 1)
        def _():
            ring_copy(way, piece, False).start()

        twin_copy(way, piece, False).start()

    def ring_step(way, s):
        away, turn = lax.div(s, groups), lax.rem(s, groups)
        group = lax.rem(lax.div(CORES * r, per) + turn, groups)

        @pl.when(r - away >= 0)
        def _():
            pass_on(way, (r - away) * groups + group)

        @pl.when(jnp.logical_and(away > 0, r + away < n_rows))
        def _():
            pass_on(way, (r + away) * groups + group)

    def keep(piece):
        columns = pl.ds(pl.multiple_of((1 - core) * width, width), width)
        part = panel_ref.at[piece_rows(piece), columns]
        pltpu.make_async_copy(part, part, twin_recv.at[piece]).wait()

        @pl.when(is_far(piece))
        def _():
            keep_panel(piece).start()

    def keep_step(s):
        away, turn = lax.div(s, groups), lax.rem(s, groups)
        group = lax.rem(lax.div(CORES * r, per) + turn, groups)

        @pl.when(r - away >= 0)
        def _():
            keep((r - away) * groups + group)

        @pl.when(jnp.logical_and(away > 0, r + away < n_rows))
        def _():
            keep((r + away) * groups + group)

    tiles = panel_ref.shape[1] // TILE
    early = n_rows // 2 * groups + LAG * chips

    def cross_copy(tile):
        slot = lax.rem(tile, 2)
        return pltpu.make_async_copy(
            cross_ref.at[slot],
            cross_out.at[pl.ds(pl.multiple_of(tile * TILE, TILE), TILE)],
            cross_sem.at[slot],
        )

    def left_copy(tile):
        slot = lax.rem(tile, 2)
        return pltpu.make_async_copy(
            left_ref.at[slot],
            left_out.at[pl.ds(pl.multiple_of(tile * TILE, TILE), TILE)],
            left_sem.at[slot],
        )

    def step(s, _):
        @pl.when(s < pieces)
        def _():
            own_step(s)

        for way in range(2):
            late = s - LAG * hops[way]

            @pl.when(
                jnp.logical_and(
                    jnp.logical_not(is_root),
                    jnp.logical_and(late >= 0, late < pieces),
                )
            )
            def _():
                ring_step(way, late)

        last = s - LAG * chips

        @pl.when(last >= 0)
        def _():
            keep_step(last)

        tile = s - early

        @pl.when(tile == 0)
        def _():
            high, low = split(own_ref[near, :])
            right_ref[pl.ds(0, near_depth), :] = low
            right_ref[pl.ds(near_depth, near_depth), :] = high
            near_copy().start()

        @pl.when(jnp.logical_and(tile >= 0, tile < tiles))
        def _():
            slot = lax.rem(tile, 2)

            @pl.when(tile >= 2)
            def _():
                cross_copy(tile - 2).wait()
                left_copy(tile - 2).wait()

            columns = pl.ds(pl.multiple_of(tile * TILE, TILE), TILE)
            high, low = split(panel_ref[near, columns].T)
            left_ref[slot] = high
            left_copy(tile).start()
            left = jnp.concatenate([high, low], axis=1)
            cross = jnp.dot(left, right_ref[...], preferred_element_type=jnp.float32)
            cross_ref[slot] = cross.astype(jnp.bfloat16)
            cross_copy(tile).start()

        return 0

    lax.fori_loop(0, early + max(tiles, pieces + LAG * chips - early), step, 0)
    for tile in range(max(tiles - 2, 0), tiles):
        cross_copy(tile).wait()
        left_copy(tile).wait()
    near_copy().wait()

    def drain(ref, sem):
        pltpu.make_async_copy(ref, ref, sem).wait()

    drain(own_ref.at[pl.ds(0, (n_cols - 1) * tok)], all_send)
    drain(own_ref, twin_send)
    drain(own_ref.at[pl.ds(0, near_depth)], local_sem.at[0])
    drain(panel_ref.at[pl.ds(0, near_depth)], local_sem.at[1])
    for way in range(2):
        if chips > 1:
            @pl.when(hops[way] < chips - 1)
            def _():
                drain(own_ref.at[:, pl.ds(0, half)], ring_send.at[way])

    for block in range(n_rows):
        sent = own_ref.at[pl.ds(block * n_cols * tok, n_cols * tok)]

        @pl.when(jnp.logical_and(r < n_rows - 1, block <= r))
        def _():
            drain(sent, up_send.at[block])

        @pl.when(jnp.logical_and(r > 0, block >= r))
        def _():
            drain(sent, down_send.at[block])


def gather(x, n_rows, n_cols):
    tok, features = x.shape
    width = features // n_cols
    total = tok * n_rows * n_cols
    groups = GROUPS if n_cols % GROUPS == 0 else n_cols
    pieces = n_rows * groups
    dma = pltpu.SemaphoreType.DMA
    return pl.pallas_call(
        functools.partial(gather_kernel, n_rows, n_cols, groups),
        out_shape=(
            jax.ShapeDtypeStruct((total // 2, width), jnp.float32),
            jax.ShapeDtypeStruct((total // 2, CORES * width), jnp.float32),
            jax.ShapeDtypeStruct((CORES * width, width), jnp.bfloat16),
            jax.ShapeDtypeStruct((total // 2, width), jnp.bfloat16),
            jax.ShapeDtypeStruct((CORES * width, total // 2), jnp.bfloat16),
        ),
        in_specs=[pl.BlockSpec(memory_space=pl.ANY)],
        out_specs=(pl.BlockSpec(memory_space=pl.ANY),) * 5,
        scratch_shapes=[
            pltpu.VMEM((total, width), jnp.float32),
            pltpu.VMEM((total, CORES * width), jnp.float32),
            pltpu.VMEM((total, width), jnp.bfloat16),
            pltpu.VMEM((2, TILE, width), jnp.bfloat16),
            pltpu.VMEM((2, TILE, total // 2), jnp.bfloat16),
            dma((2,)), dma((2,)), dma,
            dma, dma((n_cols,)),
            dma((n_rows,)), dma((n_rows,)), dma((pieces,)),
            dma((2,)), dma((2, pieces)),
            dma, dma((pieces,)),
            dma((2,)),
        ],
        compiler_params=pltpu.CompilerParams(
            collective_id=0, has_side_effects=True, vmem_limit_bytes=VMEM_LIMIT
        ),
        name="gather_columns",
    )(x)


def gram_kernel(scale, left_ref, panel_ref, near_ref, own_ref, cross_ref, out_ref, right):
    half = own_ref.shape[0]

    @pl.when(pl.program_id(0) == 0)
    def _():
        high, low = split(own_ref[...])
        right[pl.ds(0, half), :] = near_ref[...]
        right[pl.ds(half, half), :] = high
        right[pl.ds(2 * half, half), :] = low
        right[pl.ds(3 * half, half), :] = high

    high, low = split(panel_ref[...].T)
    left = jnp.concatenate([left_ref[...], high, high, low], axis=1)
    product = jnp.dot(left, right[...], preferred_element_type=jnp.float32)
    out_ref[...] = (product + cross_ref[...].astype(jnp.float32)) * scale


def gram(own, panel, cross, near, left):
    half, width = own.shape
    count = panel.shape[1]
    once = pl.Buffered(1)
    return pl.pallas_call(
        functools.partial(gram_kernel, 0.5 / half),
        grid=(count // TILE,),
        out_shape=jax.ShapeDtypeStruct((count, width), jnp.float32),
        in_specs=[
            pl.BlockSpec((TILE, half), lambda i: (i, 0)),
            pl.BlockSpec((half, TILE), lambda i: (0, i)),
            pl.BlockSpec((half, width), lambda i: (0, 0), pipeline_mode=once),
            pl.BlockSpec((half, width), lambda i: (0, 0), pipeline_mode=once),
            pl.BlockSpec((TILE, width), lambda i: (i, 0)),
        ],
        out_specs=pl.BlockSpec((TILE, width), lambda i: (i, 0)),
        scratch_shapes=[pltpu.VMEM((4 * half, width), jnp.bfloat16)],
        compiler_params=pltpu.CompilerParams(vmem_limit_bytes=VMEM_LIMIT),
        cost_estimate=pl.CostEstimate(
            flops=8 * half * width * count,
            bytes_accessed=6 * (width * count + half * (width + count)),
            transcendentals=0,
        ),
        name="gram_blocks",
    )(left, panel, near, own, cross)


def shards(x):
    n_rows, n_cols = lax.axis_size("row"), lax.axis_size("col")
    own, panel, cross, near, left = gather(x, n_rows, n_cols)
    depth = 2 * own.shape[0]
    if depth & (depth - 1):
        raise ValueError("token count")
    return gram(own, panel, cross, near, left)


def solution(mesh):
    if mesh.shape["col"] != CORES * mesh.shape["row"]:
        raise ValueError("mesh shape")
    placed = (P(("row", "col"), None),)
    return jax.shard_map(
        shards, mesh=mesh, in_specs=placed, out_specs=P("row", "col"), check_vma=False
    )
```

```python
import functools

import jax
import jax.numpy as jnp
from jax import lax
from jax.experimental import pallas as pl
from jax.experimental.pallas import tpu as pltpu
from jax.sharding import PartitionSpec as P

MESH = pl.DeviceIdType.MESH
CORES = 2
GROUPS = 8
LAG = 2
TILE = 512
VMEM_LIMIT = 56 * 2**20


def bits_of(chips):
    return max(chips.bit_length() - 1, 0)


def chip_at(place, chips):
    total = 0
    for k in range(bits_of(chips)):
        total += 2**k * lax.rem(lax.div(place, 2**k) + lax.div(place, 2 ** (k + 1)), 2)
    return total


def place_of(chip, chips):
    total, above = 0, 0
    for k in reversed(range(bits_of(chips))):
        above = lax.rem(above + lax.rem(lax.div(chip, 2**k), 2), 2)
        total += 2**k * above
    return total


def split(x):
    high = x.astype(jnp.bfloat16)
    low = (x - high.astype(jnp.float32)).astype(jnp.bfloat16)
    return high, low


def gather_kernel(
    n_rows, n_cols, groups, x_ref, own_out, panel_out, cross_out, near_out, left_out,
    own_ref, panel_ref, right_ref, cross_ref, left_ref, cross_sem, left_sem, near_sem,
    all_send, all_recv, up_send, down_send, chain_recv,
    ring_send, ring_recv, twin_send, twin_recv, local_sem,
):
    r, c = lax.axis_index("row"), lax.axis_index("col")
    chips = n_cols // CORES
    chip, core = lax.div(c, CORES), lax.rem(c, CORES)
    twin = c + 1 - 2 * core
    tok = x_ref.shape[0]
    width = own_ref.shape[1]
    half = width // 2
    per = n_cols // groups
    rows = tok * per
    pieces = n_rows * groups
    place, root = place_of(chip, chips), place_of(r, chips)
    is_root = chip == r
    follow = CORES * chip_at(lax.rem(place + 1, chips), chips) + core
    before = CORES * chip_at(lax.rem(place + chips - 1, chips), chips) + core
    ring_to = (follow, before)
    hops = (
        lax.rem(place - root + chips, chips),
        lax.rem(root - place + chips, chips),
    )

    barrier = pltpu.get_barrier_semaphore()

    def greet(k, _):
        pl.semaphore_signal(
            barrier, inc=1, device_id=(r, lax.rem(c + k, n_cols)), device_id_type=MESH
        )
        return 0

    lax.fori_loop(1, n_cols, greet, 0)

    @pl.when(r > 0)
    def _():
        pl.semaphore_signal(barrier, inc=1, device_id=(r - 1, c), device_id_type=MESH)

    @pl.when(r < n_rows - 1)
    def _():
        pl.semaphore_signal(barrier, inc=1, device_id=(r + 1, c), device_id_type=MESH)

    above, below = (r > 0).astype(jnp.int32), (r < n_rows - 1).astype(jnp.int32)
    pl.semaphore_wait(barrier, n_cols - 1 + above + below)

    def token_rows(source):
        return pl.ds(pl.multiple_of((r * n_cols + source) * tok, tok), tok)

    def x_columns(block):
        return pl.ds(pl.multiple_of(block * width, width), width)

    def piece_rows(piece):
        return pl.ds(pl.multiple_of(piece * rows, rows), rows)

    def panel_columns(way, of_core):
        return pl.ds(pl.multiple_of(of_core * width + way * half, half), half)

    def all_copy(k):
        other = lax.rem(c + k, n_cols)
        return pltpu.make_async_remote_copy(
            src_ref=x_ref.at[:, x_columns(other)],
            dst_ref=own_ref.at[token_rows(c)],
            send_sem=all_send,
            recv_sem=all_recv.at[c],
            device_id=(r, other),
            device_id_type=MESH,
        )

    def chain_copy(piece, step):
        block = own_ref.at[piece_rows(piece)]
        return pltpu.make_async_remote_copy(
            src_ref=block,
            dst_ref=block,
            send_sem=(up_send if step > 0 else down_send).at[lax.div(piece, groups)],
            recv_sem=chain_recv.at[piece],
            device_id=(r + step, c),
            device_id_type=MESH,
        )

    def panel_part(way, piece):
        return panel_ref.at[piece_rows(piece), panel_columns(way, core)]

    def ring_copy(way, piece, from_own):
        source = panel_part(way, piece)
        if from_own:
            source = own_ref.at[piece_rows(piece), pl.ds(way * half, half)]
        return pltpu.make_async_remote_copy(
            src_ref=source,
            dst_ref=panel_part(way, piece),
            send_sem=ring_send.at[way],
            recv_sem=ring_recv.at[way, piece],
            device_id=(r, ring_to[way]),
            device_id_type=MESH,
        )

    def twin_copy(way, piece, from_own):
        source = panel_part(way, piece)
        if from_own:
            source = own_ref.at[piece_rows(piece), pl.ds(way * half, half)]
        return pltpu.make_async_remote_copy(
            src_ref=source,
            dst_ref=panel_part(way, piece),
            send_sem=twin_send,
            recv_sem=twin_recv.at[piece],
            device_id=(r, twin),
            device_id_type=MESH,
        )

    def local_copy(piece):
        columns = pl.ds(pl.multiple_of(core * width, width), width)
        panel_ref[piece_rows(piece), columns] = own_ref[piece_rows(piece), :]

    near_depth = own_ref.shape[0] // 2
    near_side = lax.div(r, n_rows // 2)
    far_side = 1 - near_side
    near = pl.ds(pl.multiple_of(near_side * near_depth, near_depth), near_depth)

    def is_far(piece):
        return lax.div(piece, pieces // 2) == far_side

    def far_rows(piece):
        return piece_rows(piece - far_side * (pieces // 2))

    def keep_own(piece):
        return pltpu.make_async_copy(
            own_ref.at[piece_rows(piece)],
            own_out.at[far_rows(piece)],
            local_sem.at[0],
        )

    def keep_panel(piece):
        return pltpu.make_async_copy(
            panel_ref.at[piece_rows(piece)],
            panel_out.at[far_rows(piece)],
            local_sem.at[1],
        )

    def near_copy():
        return pltpu.make_async_copy(
            right_ref.at[pl.ds(near_depth, near_depth)], near_out, near_sem
        )

    def own_columns():
        return pltpu.make_async_copy(
            x_ref.at[:, x_columns(c)], own_ref.at[token_rows(c)], all_recv.at[c]
        )

    own_columns().start()

    def send_all(k, _):
        all_copy(k).start()
        return 0

    lax.fori_loop(1, n_cols, send_all, 0)

    def from_root(piece):
        @pl.when(is_far(piece))
        def _():
            keep_own(piece).start()

        @pl.when(is_root)
        def _():
            for way in range(2):
                if chips > 1:
                    ring_copy(way, piece, True).start()
            for way in range(2):
                twin_copy(way, piece, True).start()
            local_copy(piece)

    def own_step(s):
        away, turn = lax.div(s, groups), lax.rem(s, groups)
        group = lax.rem(lax.div(CORES * chip, per) + turn, groups)

        @pl.when(away == 0)
        def _():
            for k in range(per):
                source = group * per + k
                block = own_ref.at[token_rows(source)]
                pltpu.make_async_copy(block, block, all_recv.at[source]).wait()
            piece = r * groups + group

            @pl.when(r > 0)
            def _():
                chain_copy(piece, -1).start()

            @pl.when(r < n_rows - 1)
            def _():
                chain_copy(piece, 1).start()

            from_root(piece)

        @pl.when(jnp.logical_and(away > 0, r - away >= 0))
        def _():
            piece = (r - away) * groups + group
            chain_copy(piece, 1).wait_recv()

            @pl.when(r < n_rows - 1)
            def _():
                chain_copy(piece, 1).start()

            from_root(piece)

        @pl.when(jnp.logical_and(away > 0, r + away < n_rows))
        def _():
            piece = (r + away) * groups + group
            chain_copy(piece, -1).wait_recv()

            @pl.when(r > 0)
            def _():
                chain_copy(piece, -1).start()

            from_root(piece)

    def pass_on(way, piece):
        ring_copy(way, piece, False).wait_recv()

        @pl.when(hops[way] < chips - 1)
        def _():
            ring_copy(way, piece, False).start()

        twin_copy(way, piece, False).start()

    def ring_step(way, s):
        away, turn = lax.div(s, groups), lax.rem(s, groups)
        group = lax.rem(lax.div(CORES * r, per) + turn, groups)

        @pl.when(r - away >= 0)
        def _():
            pass_on(way, (r - away) * groups + group)

        @pl.when(jnp.logical_and(away > 0, r + away < n_rows))
        def _():
            pass_on(way, (r + away) * groups + group)

    def keep(piece):
        columns = pl.ds(pl.multiple_of((1 - core) * width, width), width)
        part = panel_ref.at[piece_rows(piece), columns]
        pltpu.make_async_copy(part, part, twin_recv.at[piece]).wait()

        @pl.when(is_far(piece))
        def _():
            keep_panel(piece).start()

    def keep_step(s):
        away, turn = lax.div(s, groups), lax.rem(s, groups)
        group = lax.rem(lax.div(CORES * r, per) + turn, groups)

        @pl.when(r - away >= 0)
        def _():
            keep((r - away) * groups + group)

        @pl.when(jnp.logical_and(away > 0, r + away < n_rows))
        def _():
            keep((r + away) * groups + group)

    tiles = panel_ref.shape[1] // TILE
    early = n_rows // 2 * groups + LAG * chips

    def cross_copy(tile):
        slot = lax.rem(tile, 2)
        return pltpu.make_async_copy(
            cross_ref.at[slot],
            cross_out.at[pl.ds(pl.multiple_of(tile * TILE, TILE), TILE)],
            cross_sem.at[slot],
        )

    def left_copy(tile):
        slot = lax.rem(tile, 2)
        return pltpu.make_async_copy(
            left_ref.at[slot],
            left_out.at[pl.ds(pl.multiple_of(tile * TILE, TILE), TILE)],
            left_sem.at[slot],
        )

    def step(s, _):
        @pl.when(s < pieces)
        def _():
            own_step(s)

        for way in range(2):
            late = s - LAG * hops[way]

            @pl.when(
                jnp.logical_and(
                    jnp.logical_not(is_root),
                    jnp.logical_and(late >= 0, late < pieces),
                )
            )
            def _():
                ring_step(way, late)

        last = s - LAG * chips

        @pl.when(last >= 0)
        def _():
            keep_step(last)

        tile = s - early

        @pl.when(tile == 0)
        def _():
            high, low = split(own_ref[near, :])
            right_ref[pl.ds(0, near_depth), :] = low
            right_ref[pl.ds(near_depth, near_depth), :] = high
            near_copy().start()

        @pl.when(jnp.logical_and(tile >= 0, tile < tiles))
        def _():
            slot = lax.rem(tile, 2)

            @pl.when(tile >= 2)
            def _():
                cross_copy(tile - 2).wait()
                left_copy(tile - 2).wait()

            columns = pl.ds(pl.multiple_of(tile * TILE, TILE), TILE)
            high, low = split(panel_ref[near, columns].T)
            left_ref[slot] = high
            left_copy(tile).start()
            left = jnp.concatenate([high, low], axis=1)
            cross = jnp.dot(left, right_ref[...], preferred_element_type=jnp.float32)
            cross_ref[slot] = cross.astype(jnp.bfloat16)
            cross_copy(tile).start()

        return 0

    lax.fori_loop(0, early + max(tiles, pieces + LAG * chips - early), step, 0)
    for tile in range(max(tiles - 2, 0), tiles):
        cross_copy(tile).wait()
        left_copy(tile).wait()
    near_copy().wait()

    def drain(ref, sem):
        pltpu.make_async_copy(ref, ref, sem).wait()

    drain(own_ref.at[pl.ds(0, (n_cols - 1) * tok)], all_send)
    drain(own_ref, twin_send)
    drain(own_ref.at[pl.ds(0, near_depth)], local_sem.at[0])
    drain(panel_ref.at[pl.ds(0, near_depth)], local_sem.at[1])
    for way in range(2):
        if chips > 1:
            @pl.when(hops[way] < chips - 1)
            def _():
                drain(own_ref.at[:, pl.ds(0, half)], ring_send.at[way])

    for block in range(n_rows):
        sent = own_ref.at[pl.ds(block * n_cols * tok, n_cols * tok)]

        @pl.when(jnp.logical_and(r < n_rows - 1, block <= r))
        def _():
            drain(sent, up_send.at[block])

        @pl.when(jnp.logical_and(r > 0, block >= r))
        def _():
            drain(sent, down_send.at[block])


def gather(x, n_rows, n_cols):
    tok, features = x.shape
    width = features // n_cols
    total = tok * n_rows * n_cols
    groups = GROUPS if n_cols % GROUPS == 0 else n_cols
    pieces = n_rows * groups
    dma = pltpu.SemaphoreType.DMA
    return pl.pallas_call(
        functools.partial(gather_kernel, n_rows, n_cols, groups),
        out_shape=(
            jax.ShapeDtypeStruct((total // 2, width), jnp.float32),
            jax.ShapeDtypeStruct((total // 2, CORES * width), jnp.float32),
            jax.ShapeDtypeStruct((CORES * width, width), jnp.bfloat16),
            jax.ShapeDtypeStruct((total // 2, width), jnp.bfloat16),
            jax.ShapeDtypeStruct((CORES * width, total // 2), jnp.bfloat16),
        ),
        in_specs=[pl.BlockSpec(memory_space=pl.ANY)],
        out_specs=(pl.BlockSpec(memory_space=pl.ANY),) * 5,
        scratch_shapes=[
            pltpu.VMEM((total, width), jnp.float32),
            pltpu.VMEM((total, CORES * width), jnp.float32),
            pltpu.VMEM((total, width), jnp.bfloat16),
            pltpu.VMEM((2, TILE, width), jnp.bfloat16),
            pltpu.VMEM((2, TILE, total // 2), jnp.bfloat16),
            dma((2,)), dma((2,)), dma,
            dma, dma((n_cols,)),
            dma((n_rows,)), dma((n_rows,)), dma((pieces,)),
            dma((2,)), dma((2, pieces)),
            dma, dma((pieces,)),
            dma((2,)),
        ],
        compiler_params=pltpu.CompilerParams(
            collective_id=0, has_side_effects=True, vmem_limit_bytes=VMEM_LIMIT
        ),
        name="gather_columns",
    )(x)


def gram_kernel(scale, left_ref, panel_ref, near_ref, own_ref, cross_ref, out_ref, right):
    half = own_ref.shape[0]

    @pl.when(pl.program_id(0) == 0)
    def _():
        high, low = split(own_ref[...])
        right[pl.ds(0, half), :] = near_ref[...]
        right[pl.ds(half, half), :] = high
        right[pl.ds(2 * half, half), :] = low
        right[pl.ds(3 * half, half), :] = high

    high, low = split(panel_ref[...].T)
    left = jnp.concatenate([left_ref[...], high, high, low], axis=1)
    for start in range(0, out_ref.shape[1], TILE):
        part = pl.ds(start, TILE)
        product = jnp.dot(left, right[:, part], preferred_element_type=jnp.float32)
        out_ref[:, part] = (product + cross_ref[:, part].astype(jnp.float32)) * scale


def gram(own, panel, cross, near, left):
    half, width = own.shape
    count = panel.shape[1]
    once = pl.Buffered(1)
    return pl.pallas_call(
        functools.partial(gram_kernel, 0.5 / half),
        grid=(count // TILE,),
        out_shape=jax.ShapeDtypeStruct((count, width), jnp.float32),
        in_specs=[
            pl.BlockSpec((TILE, half), lambda i: (i, 0)),
            pl.BlockSpec((half, TILE), lambda i: (0, i)),
            pl.BlockSpec((half, width), lambda i: (0, 0), pipeline_mode=once),
            pl.BlockSpec((half, width), lambda i: (0, 0), pipeline_mode=once),
            pl.BlockSpec((TILE, width), lambda i: (i, 0)),
        ],
        out_specs=pl.BlockSpec((TILE, width), lambda i: (i, 0)),
        scratch_shapes=[pltpu.VMEM((4 * half, width), jnp.bfloat16)],
        compiler_params=pltpu.CompilerParams(vmem_limit_bytes=VMEM_LIMIT),
        cost_estimate=pl.CostEstimate(
            flops=8 * half * width * count,
            bytes_accessed=6 * (width * count + half * (width + count)),
            transcendentals=0,
        ),
        name="gram_blocks",
    )(left, panel, near, own, cross)


def shards(x):
    n_rows, n_cols = lax.axis_size("row"), lax.axis_size("col")
    own, panel, cross, near, left = gather(x, n_rows, n_cols)
    depth = 2 * own.shape[0]
    if depth & (depth - 1):
        raise ValueError("token count")
    return gram(own, panel, cross, near, left)


def solution(mesh):
    if mesh.shape["col"] != CORES * mesh.shape["row"]:
        raise ValueError("mesh shape")
    placed = (P(("row", "col"), None),)
    return jax.shard_map(
        shards, mesh=mesh, in_specs=placed, out_specs=P("row", "col"), check_vma=False
    )
```

```python
import functools

import jax
import jax.numpy as jnp
from jax import lax
from jax.experimental import pallas as pl
from jax.experimental.pallas import tpu as pltpu
from jax.sharding import PartitionSpec as P

MESH = pl.DeviceIdType.MESH
CORES = 2
GROUPS = 8
LAG = 3
TILE = 512
ROWS = 256
VMEM_LIMIT = 56 * 2**20


def bits_of(chips):
    return max(chips.bit_length() - 1, 0)


def chip_at(place, chips):
    total = 0
    for k in range(bits_of(chips)):
        total += 2**k * lax.rem(lax.div(place, 2**k) + lax.div(place, 2 ** (k + 1)), 2)
    return total


def place_of(chip, chips):
    total, above = 0, 0
    for k in reversed(range(bits_of(chips))):
        above = lax.rem(above + lax.rem(lax.div(chip, 2**k), 2), 2)
        total += 2**k * above
    return total


def split(x):
    high = x.astype(jnp.bfloat16)
    low = (x - high.astype(jnp.float32)).astype(jnp.bfloat16)
    return high, low


def gather_kernel(
    n_rows, n_cols, groups, x_ref, own_out, panel_out, cross_out, near_out, left_out,
    own_ref, panel_ref, right_ref, cross_ref, left_ref, cross_sem, left_sem, near_sem,
    all_send, all_recv, up_send, down_send, chain_recv,
    ring_send, ring_recv, twin_send, twin_recv, local_sem,
):
    r, c = lax.axis_index("row"), lax.axis_index("col")
    chips = n_cols // CORES
    chip, core = lax.div(c, CORES), lax.rem(c, CORES)
    twin = c + 1 - 2 * core
    tok = x_ref.shape[0]
    width = own_ref.shape[1]
    half = width // 2
    per = n_cols // groups
    rows = tok * per
    pieces = n_rows * groups
    place, root = place_of(chip, chips), place_of(r, chips)
    is_root = chip == r
    follow = CORES * chip_at(lax.rem(place + 1, chips), chips) + core
    before = CORES * chip_at(lax.rem(place + chips - 1, chips), chips) + core
    ring_to = (follow, before)
    hops = (
        lax.rem(place - root + chips, chips),
        lax.rem(root - place + chips, chips),
    )

    barrier = pltpu.get_barrier_semaphore()

    def greet(k, _):
        pl.semaphore_signal(
            barrier, inc=1, device_id=(r, lax.rem(c + k, n_cols)), device_id_type=MESH
        )
        return 0

    lax.fori_loop(1, n_cols, greet, 0)

    @pl.when(r > 0)
    def _():
        pl.semaphore_signal(barrier, inc=1, device_id=(r - 1, c), device_id_type=MESH)

    @pl.when(r < n_rows - 1)
    def _():
        pl.semaphore_signal(barrier, inc=1, device_id=(r + 1, c), device_id_type=MESH)

    above, below = (r > 0).astype(jnp.int32), (r < n_rows - 1).astype(jnp.int32)
    pl.semaphore_wait(barrier, n_cols - 1 + above + below)

    def token_rows(source):
        return pl.ds(pl.multiple_of((r * n_cols + source) * tok, tok), tok)

    def x_columns(block):
        return pl.ds(pl.multiple_of(block * width, width), width)

    def piece_rows(piece):
        return pl.ds(pl.multiple_of(piece * rows, rows), rows)

    def panel_columns(way, of_core):
        return pl.ds(pl.multiple_of(of_core * width + way * half, half), half)

    def all_copy(k):
        other = lax.rem(c + k, n_cols)
        return pltpu.make_async_remote_copy(
            src_ref=x_ref.at[:, x_columns(other)],
            dst_ref=own_ref.at[token_rows(c)],
            send_sem=all_send,
            recv_sem=all_recv.at[c],
            device_id=(r, other),
            device_id_type=MESH,
        )

    def chain_copy(piece, step):
        block = own_ref.at[piece_rows(piece)]
        return pltpu.make_async_remote_copy(
            src_ref=block,
            dst_ref=block,
            send_sem=(up_send if step > 0 else down_send).at[lax.div(piece, groups)],
            recv_sem=chain_recv.at[piece],
            device_id=(r + step, c),
            device_id_type=MESH,
        )

    def panel_part(way, piece):
        return panel_ref.at[piece_rows(piece), panel_columns(way, core)]

    def ring_copy(way, piece, from_own):
        source = panel_part(way, piece)
        if from_own:
            source = own_ref.at[piece_rows(piece), pl.ds(way * half, half)]
        return pltpu.make_async_remote_copy(
            src_ref=source,
            dst_ref=panel_part(way, piece),
            send_sem=ring_send.at[way],
            recv_sem=ring_recv.at[way, piece],
            device_id=(r, ring_to[way]),
            device_id_type=MESH,
        )

    def twin_copy(way, piece, from_own):
        source = panel_part(way, piece)
        if from_own:
            source = own_ref.at[piece_rows(piece), pl.ds(way * half, half)]
        return pltpu.make_async_remote_copy(
            src_ref=source,
            dst_ref=panel_part(way, piece),
            send_sem=twin_send,
            recv_sem=twin_recv.at[piece],
            device_id=(r, twin),
            device_id_type=MESH,
        )

    def local_copy(piece):
        columns = pl.ds(pl.multiple_of(core * width, width), width)
        panel_ref[piece_rows(piece), columns] = own_ref[piece_rows(piece), :]

    near_depth = own_ref.shape[0] // 2
    near_side = lax.div(r, n_rows // 2)
    far_side = 1 - near_side
    near = pl.ds(pl.multiple_of(near_side * near_depth, near_depth), near_depth)

    def is_far(piece):
        return lax.div(piece, pieces // 2) == far_side

    def far_rows(piece):
        return piece_rows(piece - far_side * (pieces // 2))

    def keep_own(piece):
        return pltpu.make_async_copy(
            own_ref.at[piece_rows(piece)],
            own_out.at[far_rows(piece)],
            local_sem.at[0],
        )

    def keep_panel(piece):
        return pltpu.make_async_copy(
            panel_ref.at[piece_rows(piece)],
            panel_out.at[far_rows(piece)],
            local_sem.at[1],
        )

    def near_copy():
        return pltpu.make_async_copy(
            right_ref.at[pl.ds(near_depth, near_depth)], near_out, near_sem
        )

    def own_columns():
        return pltpu.make_async_copy(
            x_ref.at[:, x_columns(c)], own_ref.at[token_rows(c)], all_recv.at[c]
        )

    own_columns().start()

    def send_all(k, _):
        all_copy(k).start()
        return 0

    lax.fori_loop(1, n_cols, send_all, 0)

    def from_root(piece):
        @pl.when(is_far(piece))
        def _():
            keep_own(piece).start()

        @pl.when(is_root)
        def _():
            for way in range(2):
                if chips > 1:
                    ring_copy(way, piece, True).start()
            for way in range(2):
                twin_copy(way, piece, True).start()
            local_copy(piece)

    def own_step(s):
        away, turn = lax.div(s, groups), lax.rem(s, groups)
        group = lax.rem(lax.div(CORES * chip, per) + turn, groups)

        @pl.when(away == 0)
        def _():
            for k in range(per):
                source = group * per + k
                block = own_ref.at[token_rows(source)]
                pltpu.make_async_copy(block, block, all_recv.at[source]).wait()
            piece = r * groups + group

            @pl.when(r > 0)
            def _():
                chain_copy(piece, -1).start()

            @pl.when(r < n_rows - 1)
            def _():
                chain_copy(piece, 1).start()

            from_root(piece)

        @pl.when(jnp.logical_and(away > 0, r - away >= 0))
        def _():
            piece = (r - away) * groups + group
            chain_copy(piece, 1).wait_recv()

            @pl.when(r < n_rows - 1)
            def _():
                chain_copy(piece, 1).start()

            from_root(piece)

        @pl.when(jnp.logical_and(away > 0, r + away < n_rows))
        def _():
            piece = (r + away) * groups + group
            chain_copy(piece, -1).wait_recv()

            @pl.when(r > 0)
            def _():
                chain_copy(piece, -1).start()

            from_root(piece)

    def pass_on(way, piece):
        ring_copy(way, piece, False).wait_recv()

        @pl.when(hops[way] < chips - 1)
        def _():
            ring_copy(way, piece, False).start()

        twin_copy(way, piece, False).start()

    def ring_step(way, s):
        away, turn = lax.div(s, groups), lax.rem(s, groups)
        group = lax.rem(lax.div(CORES * r, per) + turn, groups)

        @pl.when(r - away >= 0)
        def _():
            pass_on(way, (r - away) * groups + group)

        @pl.when(jnp.logical_and(away > 0, r + away < n_rows))
        def _():
            pass_on(way, (r + away) * groups + group)

    def keep(piece):
        columns = pl.ds(pl.multiple_of((1 - core) * width, width), width)
        part = panel_ref.at[piece_rows(piece), columns]
        pltpu.make_async_copy(part, part, twin_recv.at[piece]).wait()

        @pl.when(is_far(piece))
        def _():
            keep_panel(piece).start()

    def keep_step(s):
        away, turn = lax.div(s, groups), lax.rem(s, groups)
        group = lax.rem(lax.div(CORES * r, per) + turn, groups)

        @pl.when(r - away >= 0)
        def _():
            keep((r - away) * groups + group)

        @pl.when(jnp.logical_and(away > 0, r + away < n_rows))
        def _():
            keep((r + away) * groups + group)

    tiles = panel_ref.shape[1] // TILE
    early = n_rows // 2 * groups + LAG * chips

    def cross_copy(tile):
        slot = lax.rem(tile, 2)
        return pltpu.make_async_copy(
            cross_ref.at[slot],
            cross_out.at[pl.ds(pl.multiple_of(tile * TILE, TILE), TILE)],
            cross_sem.at[slot],
        )

    def left_copy(tile):
        slot = lax.rem(tile, 2)
        return pltpu.make_async_copy(
            left_ref.at[slot],
            left_out.at[pl.ds(pl.multiple_of(tile * TILE, TILE), TILE)],
            left_sem.at[slot],
        )

    def step(s, _):
        @pl.when(s < pieces)
        def _():
            own_step(s)

        for way in range(2):
            late = s - LAG * hops[way]

            @pl.when(
                jnp.logical_and(
                    jnp.logical_not(is_root),
                    jnp.logical_and(late >= 0, late < pieces),
                )
            )
            def _():
                ring_step(way, late)

        last = s - LAG * chips

        @pl.when(last >= 0)
        def _():
            keep_step(last)

        tile = s - early

        @pl.when(tile == 0)
        def _():
            high, low = split(own_ref[near, :])
            right_ref[pl.ds(0, near_depth), :] = low
            right_ref[pl.ds(near_depth, near_depth), :] = high
            near_copy().start()

        @pl.when(jnp.logical_and(tile >= 0, tile < tiles))
        def _():
            slot = lax.rem(tile, 2)

            @pl.when(tile >= 2)
            def _():
                cross_copy(tile - 2).wait()
                left_copy(tile - 2).wait()

            columns = pl.ds(pl.multiple_of(tile * TILE, TILE), TILE)
            high, low = split(panel_ref[near, columns].T)
            left_ref[slot] = high
            left_copy(tile).start()
            left = jnp.concatenate([high, low], axis=1)
            cross = jnp.dot(left, right_ref[...], preferred_element_type=jnp.float32)
            cross_ref[slot] = cross.astype(jnp.bfloat16)
            cross_copy(tile).start()

        return 0

    lax.fori_loop(0, early + max(tiles, pieces + LAG * chips - early), step, 0)
    for tile in range(max(tiles - 2, 0), tiles):
        cross_copy(tile).wait()
        left_copy(tile).wait()
    near_copy().wait()

    def drain(ref, sem):
        pltpu.make_async_copy(ref, ref, sem).wait()

    drain(own_ref.at[pl.ds(0, (n_cols - 1) * tok)], all_send)
    drain(own_ref, twin_send)
    drain(own_ref.at[pl.ds(0, near_depth)], local_sem.at[0])
    drain(panel_ref.at[pl.ds(0, near_depth)], local_sem.at[1])
    for way in range(2):
        if chips > 1:
            @pl.when(hops[way] < chips - 1)
            def _():
                drain(own_ref.at[:, pl.ds(0, half)], ring_send.at[way])

    for block in range(n_rows):
        sent = own_ref.at[pl.ds(block * n_cols * tok, n_cols * tok)]

        @pl.when(jnp.logical_and(r < n_rows - 1, block <= r))
        def _():
            drain(sent, up_send.at[block])

        @pl.when(jnp.logical_and(r > 0, block >= r))
        def _():
            drain(sent, down_send.at[block])


def gather(x, n_rows, n_cols):
    tok, features = x.shape
    width = features // n_cols
    total = tok * n_rows * n_cols
    groups = GROUPS if n_cols % GROUPS == 0 else n_cols
    pieces = n_rows * groups
    dma = pltpu.SemaphoreType.DMA
    return pl.pallas_call(
        functools.partial(gather_kernel, n_rows, n_cols, groups),
        out_shape=(
            jax.ShapeDtypeStruct((total // 2, width), jnp.float32),
            jax.ShapeDtypeStruct((total // 2, CORES * width), jnp.float32),
            jax.ShapeDtypeStruct((CORES * width, width), jnp.bfloat16),
            jax.ShapeDtypeStruct((total // 2, width), jnp.bfloat16),
            jax.ShapeDtypeStruct((CORES * width, total // 2), jnp.bfloat16),
        ),
        in_specs=[pl.BlockSpec(memory_space=pl.ANY)],
        out_specs=(pl.BlockSpec(memory_space=pl.ANY),) * 5,
        scratch_shapes=[
            pltpu.VMEM((total, width), jnp.float32),
            pltpu.VMEM((total, CORES * width), jnp.float32),
            pltpu.VMEM((total, width), jnp.bfloat16),
            pltpu.VMEM((2, TILE, width), jnp.bfloat16),
            pltpu.VMEM((2, TILE, total // 2), jnp.bfloat16),
            dma((2,)), dma((2,)), dma,
            dma, dma((n_cols,)),
            dma((n_rows,)), dma((n_rows,)), dma((pieces,)),
            dma((2,)), dma((2, pieces)),
            dma, dma((pieces,)),
            dma((2,)),
        ],
        compiler_params=pltpu.CompilerParams(
            collective_id=0, has_side_effects=True, vmem_limit_bytes=VMEM_LIMIT
        ),
        name="gather_columns",
    )(x)


def gram_kernel(scale, left_ref, panel_ref, near_ref, own_ref, cross_ref, out_ref, right):
    half = own_ref.shape[0]

    @pl.when(pl.program_id(0) == 0)
    def _():
        high, low = split(own_ref[...])
        right[pl.ds(0, half), :] = near_ref[...]
        right[pl.ds(half, half), :] = high
        right[pl.ds(2 * half, half), :] = low
        right[pl.ds(3 * half, half), :] = high

    high, low = split(panel_ref[...].T)
    left = jnp.concatenate([left_ref[...], high, high, low], axis=1)
    product = jnp.dot(left, right[...], preferred_element_type=jnp.float32)
    out_ref[...] = (product + cross_ref[...].astype(jnp.float32)) * scale


def gram(own, panel, cross, near, left):
    half, width = own.shape
    count = panel.shape[1]
    once = pl.Buffered(1)
    return pl.pallas_call(
        functools.partial(gram_kernel, 0.5 / half),
        grid=(count // ROWS,),
        out_shape=jax.ShapeDtypeStruct((count, width), jnp.float32),
        in_specs=[
            pl.BlockSpec((ROWS, half), lambda i: (i, 0)),
            pl.BlockSpec((half, ROWS), lambda i: (0, i)),
            pl.BlockSpec((half, width), lambda i: (0, 0), pipeline_mode=once),
            pl.BlockSpec((half, width), lambda i: (0, 0), pipeline_mode=once),
            pl.BlockSpec((ROWS, width), lambda i: (i, 0)),
        ],
        out_specs=pl.BlockSpec((ROWS, width), lambda i: (i, 0)),
        scratch_shapes=[pltpu.VMEM((4 * half, width), jnp.bfloat16)],
        compiler_params=pltpu.CompilerParams(vmem_limit_bytes=VMEM_LIMIT),
        cost_estimate=pl.CostEstimate(
            flops=8 * half * width * count,
            bytes_accessed=6 * (width * count + half * (width + count)),
            transcendentals=0,
        ),
        name="gram_blocks",
    )(left, panel, near, own, cross)


def shards(x):
    n_rows, n_cols = lax.axis_size("row"), lax.axis_size("col")
    own, panel, cross, near, left = gather(x, n_rows, n_cols)
    depth = 2 * own.shape[0]
    if depth & (depth - 1):
        raise ValueError("token count")
    return gram(own, panel, cross, near, left)


def solution(mesh):
    if mesh.shape["col"] != CORES * mesh.shape["row"]:
        raise ValueError("mesh shape")
    placed = (P(("row", "col"), None),)
    return jax.shard_map(
        shards, mesh=mesh, in_specs=placed, out_specs=P("row", "col"), check_vma=False
    )
```
